256 devices in a mesh: pipe: 16 (over x_hi, y, core), dp: 16 (over z, x_lo).
Axes of the slice: x: 4 (x_hi: 2, x_lo: 2; x = x_hi * 2 + x_lo), y: 4, z: 8, core: 2. Of those that a mesh axis runs over, the one named last changes fastest.
Arguments:
- fwd_in: bfloat16 [16, 1024, 3200], P('pipe', 'dp'), may hold values from -6 to 6
- fwd_ids: int32 [16, 1024], P('pipe', 'dp'), may hold values from 0 to 15, as said below
- fwd_lengths: int32 [16, 16], P('pipe', 'dp'), may hold values from 1 to 64
- bwd_in: bfloat16 [16, 1024, 3200], P('pipe', 'dp'), may hold values from -6 to 6
- bwd_grad: bfloat16 [16, 1024, 3200], P('pipe', 'dp'), may hold values from -6 to 6
- bwd_ids: int32 [16, 1024], P('pipe', 'dp'), may hold values from 0 to 15, as said below
- bwd_lengths: int32 [16, 16], P('pipe', 'dp'), may hold values from 1 to 64
- norm_gain: float32 [16, 3200], P('pipe'), may hold values from 0.1 to 1.9
- router: bfloat16 [16, 3200], P('pipe'), may hold values from -0.109375 to 0.109375
- w_gate: bfloat16 [16, 3200, 9216], P('pipe', None, 'dp'), may hold values from -0.109375 to 0.109375
- w_up: bfloat16 [16, 3200, 9216], P('pipe', None, 'dp'), may hold values from -0.109375 to 0.109375
- w_down: bfloat16 [16, 9216, 3200], P('pipe', 'dp'), may hold values from -0.0625 to 0.0625
Outputs:
- fwd_out: bfloat16 [16, 1024, 3200], P('pipe', 'dp')
- bwd_out: bfloat16 [16, 1024, 3200], P('pipe', 'dp')
The draws below stay inside these ranges and needn't reach their ends.
Inputs may be any that keep to these rules, and one draw needn't show every extreme that they name: `fwd_ids`: expert 0 is the one held in this window. In the 64 tokens of one device at one section, between 1 and 8 tokens name expert 0; in every section some device has exactly 8, and in some section every device has 8. `bwd_ids`: like fwd_ids.
All inputs are finite; a program needn't handle non-finite values.
Results may differ from the reference program's by a relative error of at most 0.008.
Values may be sent and summed in bfloat16 or wider, within the bound.
No kernel may reach another device: no remote copies, remote signals or barrier semaphores. Data moves between devices by JAX's collectives and lax.ppermute only.
A program may use at most 64 MiB of HBM per device.

```python
import jax
import jax.numpy as jnp
from jax import lax

D = 3200
FW = 9216
TOK = 64
EXPERTS = 16
CAP = 8
TOKENS = 1024
N_PIPE = 16
N_DP = 16


def route_draw(key):
    keys = jax.random.split(key, 5)
    counts = jax.random.randint(keys[0], (N_PIPE, N_DP), 1, CAP + 1)
    busiest = jax.random.randint(keys[1], (N_PIPE,), 0, N_DP)
    devices = jnp.arange(N_DP, dtype=jnp.int32)[None, :]
    counts = jnp.where(devices == busiest[:, None], CAP, counts)
    full_section = jax.random.randint(keys[2], (), 0, N_PIPE)
    sections = jnp.arange(N_PIPE, dtype=jnp.int32)[:, None]
    counts = jnp.where(sections == full_section, CAP, counts)
    block_keys = jax.random.split(keys[3], N_PIPE * N_DP)
    orders = jax.vmap(lambda k: jax.random.permutation(k, TOK))(block_keys).reshape(N_PIPE, N_DP, TOK)
    others = jax.random.randint(keys[4], (N_PIPE, N_DP, TOK), 1, EXPERTS)
    ids = jnp.where(orders < counts[:, :, None], 0, others)
    return ids.reshape(N_PIPE, N_DP * TOK).astype(jnp.int32)


def draw_fwd_ids(key, part):
    key = jax.random.fold_in(key, 11)
    return route_draw(key)


def draw_bwd_ids(key, part):
    key = jax.random.fold_in(key, 23)
    return route_draw(key)


def place_ends(entries, stream_key, least, largest):
    extent = entries.shape
    index_at = [jax.random.randint(jax.random.fold_in(stream_key, axis), (), 0, extent[axis]) for axis in range(len(extent))]
    entries = entries.at[tuple(index_at)].set(least)
    longest = extent.index(max(extent))
    index_at[longest] = (index_at[longest] + 1) % extent[longest]
    return entries.at[tuple(index_at)].set(largest)


def shard_levels(own_key, shape, shards, low, largest):
    def one(axis_at, blocks):
        draws = jax.random.uniform(jax.random.fold_in(jax.random.fold_in(own_key, 6), axis_at), (blocks,), jnp.float32, low / len(shards), largest / len(shards))
        return jnp.repeat(jnp.exp(draws), shape[axis_at] // blocks).reshape((-1,) + (1,) * (len(shape) - axis_at - 1))

    level = one(*shards[0])
    for cut in shards[1:]:
        level = level * one(*cut)
    return level


def noise(stream_key, dims, spread, bound, cuts=(), kind=jnp.bfloat16):
    result = jax.random.normal(stream_key, dims, jnp.float32) * spread
    if len(cuts) > 0:
        result = shard_levels(stream_key, dims, cuts, -0.22, 0.18) * result
    return jnp.clip(result, min=-bound, max=bound).astype(kind)


def setup_inputs(seed: int = 0) -> dict:
    seeds = jax.random.split(jax.random.key(seed), 13)
    fwd_in = noise(seeds[0], (N_PIPE, TOKENS, D), 1.0, 6.0, ((0, 16), (1, 16)))
    fwd_ids = draw_fwd_ids(jax.random.fold_in(seeds[12], 71), 0)
    fwd_lengths = place_ends(jax.random.randint(seeds[2], (N_PIPE, N_DP), 1, TOK + 1), jax.random.fold_in(seeds[2], 1), 1, TOK).astype(jnp.int32)
    bwd_in = noise(seeds[3], (N_PIPE, TOKENS, D), 1.0, 6.0, ((0, 16), (1, 16)))
    bwd_grad = noise(seeds[4], (N_PIPE, TOKENS, D), 1.0, 6.0, ((0, 16), (1, 16)))
    bwd_ids = draw_bwd_ids(jax.random.fold_in(seeds[12], 71), 0)
    bwd_lengths = place_ends(jax.random.randint(seeds[6], (N_PIPE, N_DP), 1, TOK + 1), jax.random.fold_in(seeds[6], 1), 1, TOK).astype(jnp.int32)
    norm_gain = jnp.clip(1.0 + 0.18 * jax.random.normal(seeds[7], (N_PIPE, D), jnp.float32), 0.1, 1.9)
    router = noise(seeds[8], (N_PIPE, D), D ** -0.5, 0.109375, ((0, 16),))
    w_gate = noise(seeds[9], (N_PIPE, D, FW), D ** -0.5, 0.109375, ((0, 16), (2, 16)))
    w_up = noise(seeds[10], (N_PIPE, D, FW), D ** -0.5, 0.109375, ((0, 16), (2, 16)))
    w_down = noise(seeds[11], (N_PIPE, FW, D), FW ** -0.5, 0.0625, ((0, 16), (1, 16)))
    return dict(fwd_in=fwd_in, fwd_ids=fwd_ids, fwd_lengths=fwd_lengths, bwd_in=bwd_in, bwd_grad=bwd_grad, bwd_ids=bwd_ids, bwd_lengths=bwd_lengths, norm_gain=norm_gain, router=router, w_gate=w_gate, w_up=w_up, w_down=w_down)


EPS = 1e-05

def normalize(tokens, norm_w):
    values = tokens.astype(jnp.float32)
    inv_scale = lax.rsqrt(lax.optimization_barrier(jnp.mean(values * values, axis=-1, keepdims=True)) + EPS)
    return (values, inv_scale, (values * inv_scale * norm_w).astype(jnp.bfloat16))

def slot_targets(route_ids):
    chosen = (route_ids == 0).astype(jnp.int32)
    slot_rank = jnp.cumsum(chosen, axis=1) - 1
    source = jnp.arange(N_DP, dtype=jnp.int32)[:, None]
    target = jnp.where(chosen == 1, source * CAP + slot_rank, N_DP * CAP)
    return target.reshape(-1).astype(jnp.int32)

def scatter_rows(rows, target):
    buffer = jnp.zeros((N_DP * CAP + 1, rows.shape[1]), rows.dtype)
    return buffer.at[target].set(rows)[:-1]

def gather_rows(buffer, target):
    padded = jnp.concatenate([buffer, jnp.zeros((1, buffer.shape[1]), buffer.dtype)], axis=0)
    return padded[target]

def expert_hidden(slot_rows, gate_w, up_w):
    gate_pre = jnp.dot(slot_rows, gate_w, preferred_element_type=jnp.float32)
    up_pre = jnp.dot(slot_rows, up_w, preferred_element_type=jnp.float32)
    hidden = (gate_pre * jax.nn.sigmoid(gate_pre) * up_pre).astype(jnp.bfloat16)
    return (gate_pre, up_pre, hidden)

def section(inputs):
    fwd_rows, fwd_route, fwd_len, bwd_rows, bwd_grads, bwd_route, bwd_len, norm_w, router_w, gate_w, up_w, down_w = inputs
    positions = jnp.arange(TOK, dtype=jnp.int32)[None, :]
    f_values, f_inv, f_normed = normalize(fwd_rows, norm_w)
    f_target = slot_targets(fwd_route.reshape(N_DP, TOK))
    f_mask = (positions < fwd_len[:, None]).astype(jnp.float32).reshape(-1)
    f_prob = jax.nn.sigmoid(jnp.dot(f_normed, router_w, preferred_element_type=jnp.float32))
    f_buffer = scatter_rows(f_normed, f_target)
    gate_pre, up_pre, hidden = expert_hidden(f_buffer, gate_w, up_w)
    f_result = jnp.dot(hidden, down_w, preferred_element_type=jnp.float32).astype(jnp.bfloat16)
    f_back = gather_rows(f_result, f_target).astype(jnp.float32)
    layer_out = (f_values + (f_mask * f_prob)[:, None] * f_back).astype(jnp.bfloat16)
    b_values, b_inv, b_normed = normalize(bwd_rows, norm_w)
    b_target = slot_targets(bwd_route.reshape(N_DP, TOK))
    b_mask = (positions < bwd_len[:, None]).astype(jnp.float32).reshape(-1)
    b_prob = jax.nn.sigmoid(jnp.dot(b_normed, router_w, preferred_element_type=jnp.float32))
    grad32 = bwd_grads.astype(jnp.float32)
    scaled_grad = (grad32 * b_mask[:, None]).astype(jnp.bfloat16)
    b_buffer = scatter_rows(b_normed, b_target)
    g_buffer = scatter_rows(scaled_grad, b_target)
    gate_pre, up_pre, hidden = expert_hidden(b_buffer, gate_w, up_w)
    d_hidden = lax.dot_general(g_buffer, down_w, (((1,), (1,)), ((), ())), preferred_element_type=jnp.float32)
    row_dot = lax.optimization_barrier(jnp.sum(hidden.astype(jnp.float32) * d_hidden, axis=1))
    gate_sig = jax.nn.sigmoid(gate_pre)
    d_gate = (d_hidden * up_pre * gate_sig * (1.0 + gate_pre * (1.0 - gate_sig))).astype(jnp.bfloat16)
    d_up = (d_hidden * gate_pre * gate_sig).astype(jnp.bfloat16)
    d_rows = (lax.dot_general(d_gate, gate_w, (((1,), (1,)), ((), ())), preferred_element_type=jnp.float32) + lax.dot_general(d_up, up_w, (((1,), (1,)), ((), ())), preferred_element_type=jnp.float32)).astype(jnp.bfloat16)
    d_tok = gather_rows(d_rows, b_target).astype(jnp.float32)
    dot_tok = gather_rows(row_dot[:, None], b_target)[:, 0]
    d_logit = b_mask * dot_tok * b_prob * (1.0 - b_prob)
    d_normed = b_prob[:, None] * d_tok + d_logit[:, None] * router_w.astype(jnp.float32)[None, :]
    weighted = norm_w * d_normed
    inner = lax.optimization_barrier(jnp.mean(weighted * b_values, axis=-1, keepdims=True))
    d_input = grad32 + b_inv * weighted - b_values * b_inv * b_inv * b_inv * inner
    return (layer_out, d_input.astype(jnp.bfloat16))

def reference(fwd_in, fwd_ids, fwd_lengths, bwd_in, bwd_grad, bwd_ids, bwd_lengths, norm_gain, router, w_gate, w_up, w_down):
    layer_outs, input_grads = lax.map(section, (fwd_in, fwd_ids, fwd_lengths, bwd_in, bwd_grad, bwd_ids, bwd_lengths, norm_gain, router, w_gate, w_up, w_down))
    return (jnp.roll(layer_outs, 1, axis=0), jnp.roll(input_grads, -1, axis=0))
```

```python
import jax
import jax.numpy as jnp
from jax import lax
from jax.sharding import PartitionSpec as P

EXPERTS = 16


EPS = 1e-05


def shifted(value, axis, steps):
    count = lax.axis_size(axis)
    pairs = [(source, (source + steps) % count) for source in range(count)]
    return lax.ppermute(value, axis, pairs)


def slot_of(route_ids, capacity):
    chosen = (route_ids == 0).astype(jnp.int32)
    return jnp.where(chosen == 1, jnp.cumsum(chosen) - 1, capacity)


def placement_matrix(target, capacity):
    return (target[None, :] == jnp.arange(capacity, dtype=jnp.int32)[:, None]).astype(jnp.bfloat16)


def pack_rows(placing, tok_rows):
    return jnp.dot(placing, tok_rows, preferred_element_type=jnp.float32)


def overlay(placing, rows, tokens):
    placed = lax.dot_general(
        placing, rows, (((0,), (0,)), ((), ())), preferred_element_type=jnp.float32
    ).astype(jnp.bfloat16)
    chosen = jnp.sum(placing.astype(jnp.float32), axis=0) > 0
    return jnp.where(chosen[:, None], placed, tokens)


def normalize(values, norm_w):
    inv_scale = lax.rsqrt(jnp.mean(values * values, axis=-1, keepdims=True) + EPS)
    return (inv_scale, (values * inv_scale * norm_w).astype(jnp.bfloat16))


def exchange(blocks):
    return lax.all_to_all(blocks, "dp", 0, 0, tiled=False)


def body(
    fwd_in,
    fwd_ids,
    fwd_lengths,
    bwd_in,
    bwd_grad,
    bwd_ids,
    bwd_lengths,
    norm_gain,
    router,
    w_gate,
    w_up,
    w_down,
):
    tok_count, width = fwd_in.shape[1:]
    capacity = max(2, 2 * tok_count // EXPERTS)
    n_dp = lax.axis_size("dp")
    norm_w = norm_gain[0]
    router_w = router[0]
    gate_w = w_gate[0]
    up_w = w_up[0]
    down_w = w_down[0]
    positions = jnp.arange(tok_count, dtype=jnp.int32)

    def hidden_parts(slot_rows):
        gate_pre = jnp.dot(slot_rows, gate_w, preferred_element_type=jnp.float32)
        up_pre = jnp.dot(slot_rows, up_w, preferred_element_type=jnp.float32)
        hidden = (gate_pre * jax.nn.sigmoid(gate_pre) * up_pre).astype(jnp.bfloat16)
        return (gate_pre, up_pre, hidden)

    def slot_side(tokens, ids, length):
        placing = placement_matrix(slot_of(ids, capacity), capacity)
        mask = (positions < length).astype(jnp.float32)
        slot_mask = jnp.sum(placing.astype(jnp.float32) * mask[None, :], axis=1)
        values = pack_rows(placing, tokens)
        inv, normed = normalize(values, norm_w)
        logit = jnp.dot(normed, router_w, preferred_element_type=jnp.float32)
        return placing, slot_mask, values, inv, normed, jax.nn.sigmoid(logit)

    next_tokens = shifted(fwd_in[0], "pipe", 1)
    next_ids = shifted(fwd_ids, "pipe", 1)
    prev_grads = shifted(bwd_grad[0], "pipe", -1)
    prev_ids = shifted(bwd_ids, "pipe", -1)

    b_place, b_mask, b_values, b_inv, b_normed, b_prob = slot_side(
        bwd_in[0], bwd_ids[0], bwd_lengths[0, 0]
    )
    g_values = pack_rows(b_place, bwd_grad[0])
    g_send = (g_values * b_mask[:, None]).astype(jnp.bfloat16)
    f_place, f_mask, f_values, f_inv, f_normed, f_prob = slot_side(
        fwd_in[0], fwd_ids[0], fwd_lengths[0, 0]
    )

    def gathered(rows):
        return exchange(jnp.broadcast_to(rows[None], (n_dp,) + rows.shape))

    bg_rows = gathered(jnp.concatenate([b_normed, g_send], axis=0))
    b_rows = bg_rows[:, :capacity].reshape(n_dp * capacity, width)
    g_rows = bg_rows[:, capacity:].reshape(n_dp * capacity, width)
    f_rows = gathered(f_normed).reshape(n_dp * capacity, width)

    gate_pre, up_pre, hidden = hidden_parts(b_rows)
    d_hidden = lax.dot_general(
        g_rows, down_w, (((1,), (1,)), ((), ())), preferred_element_type=jnp.float32
    )
    dot_part = jnp.sum(hidden.astype(jnp.float32) * d_hidden, axis=1)
    gate_sig = jax.nn.sigmoid(gate_pre)
    d_gate = (d_hidden * up_pre * gate_sig * (1.0 + gate_pre * (1.0 - gate_sig))).astype(
        jnp.bfloat16
    )
    d_up = (d_hidden * gate_pre * gate_sig).astype(jnp.bfloat16)
    d_part = lax.dot_general(
        d_gate, gate_w, (((1,), (1,)), ((), ())), preferred_element_type=jnp.float32
    )
    d_part = d_part + lax.dot_general(
        d_up, up_w, (((1,), (1,)), ((), ())), preferred_element_type=jnp.float32
    )
    dot_high = dot_part.astype(jnp.bfloat16)
    dot_low = (dot_part - dot_high.astype(jnp.float32)).astype(jnp.bfloat16)
    lanes = jnp.arange(128)[None, :]
    dot_cols = jnp.where(
        lanes == 0, dot_high[:, None], jnp.where(lanes == 1, dot_low[:, None], 0)
    ).astype(jnp.bfloat16)
    d_send = jnp.concatenate([d_part.astype(jnp.bfloat16), dot_cols], axis=1)
    d_got = exchange(d_send.reshape(n_dp, capacity, width + 128))
    d_sum = jnp.sum(d_got.astype(jnp.float32), axis=0)

    f_hidden = hidden_parts(f_rows)[2]
    f_part = jnp.dot(f_hidden, down_w, preferred_element_type=jnp.float32).astype(jnp.bfloat16)
    f_got = exchange(f_part.reshape(n_dp, capacity, width))
    f_back = jnp.sum(f_got.astype(jnp.float32), axis=0).astype(jnp.bfloat16)

    d_rows = d_sum[:, :width].astype(jnp.bfloat16).astype(jnp.float32)
    row_dot = d_sum[:, width] + d_sum[:, width + 1]
    d_logit = b_mask * row_dot * b_prob * (1.0 - b_prob)
    d_normed = b_prob[:, None] * d_rows + d_logit[:, None] * router_w.astype(jnp.float32)[None, :]
    weighted = norm_w * d_normed
    inner = jnp.mean(weighted * b_values, axis=-1, keepdims=True)
    d_input = (g_values + b_inv * weighted - b_values * b_inv * b_inv * b_inv * inner).astype(
        jnp.bfloat16
    )
    d_moved = shifted(d_input, "pipe", -1)
    layer_rows = (f_values + (f_mask * f_prob)[:, None] * f_back.astype(jnp.float32)).astype(
        jnp.bfloat16
    )
    f_moved = shifted(layer_rows, "pipe", 1)

    next_place = placement_matrix(slot_of(next_ids[0], capacity), capacity)
    prev_place = placement_matrix(slot_of(prev_ids[0], capacity), capacity)
    bwd_out = overlay(prev_place, d_moved, prev_grads)
    fwd_out = overlay(next_place, f_moved, next_tokens)
    return (fwd_out[None], bwd_out[None])


def solution(mesh):
    in_specs = (
        P("pipe", "dp", None),
        P("pipe", "dp"),
        P("pipe", "dp"),
        P("pipe", "dp", None),
        P("pipe", "dp", None),
        P("pipe", "dp"),
        P("pipe", "dp"),
        P("pipe", None),
        P("pipe", None),
        P("pipe", None, "dp"),
        P("pipe", None, "dp"),
        P("pipe", "dp", None),
    )
    out_specs = (P("pipe", "dp", None), P("pipe", "dp", None))
    return jax.shard_map(body, mesh=mesh, in_specs=in_specs, out_specs=out_specs, check_vma=False)
```

```python
import jax
import jax.numpy as jnp
from jax import lax
from jax.sharding import PartitionSpec as P

EXPERTS = 16


EPS = 1e-05


def shifted(value, axis, steps):
    count = lax.axis_size(axis)
    pairs = [(source, (source + steps) % count) for source in range(count)]
    return lax.ppermute(value, axis, pairs)


def slot_of(route_ids, capacity):
    chosen = (route_ids == 0).astype(jnp.int32)
    return jnp.where(chosen == 1, jnp.cumsum(chosen) - 1, capacity)


def placement_matrix(target, capacity):
    return (target[None, :] == jnp.arange(capacity, dtype=jnp.int32)[:, None]).astype(jnp.bfloat16)


def pack_rows(placing, tok_rows):
    return jnp.dot(placing, tok_rows, preferred_element_type=jnp.float32)


def overlay(placing, rows, tokens):
    placed = lax.dot_general(
        placing, rows, (((0,), (0,)), ((), ())), preferred_element_type=jnp.float32
    ).astype(jnp.bfloat16)
    chosen = jnp.sum(placing.astype(jnp.float32), axis=0) > 0
    return jnp.where(chosen[:, None], placed, tokens)


def normalize(values, norm_w):
    inv_scale = lax.rsqrt(jnp.mean(values * values, axis=-1, keepdims=True) + EPS)
    return (inv_scale, (values * inv_scale * norm_w).astype(jnp.bfloat16))


def along_z(value, steps):
    count = lax.axis_size("dp")
    pairs = [(source, (source + 2 * steps) % count) for source in range(count)]
    return lax.ppermute(value, "dp", pairs)


def swap_x(value):
    count = lax.axis_size("dp")
    return lax.ppermute(value, "dp", [(source, source ^ 1) for source in range(count)])


def gather_column(own):
    half = own.shape[1] // 256 * 128
    below2 = along_z(own, 2)
    above2 = along_z(own, -2)
    below1 = along_z(own, 1)
    above1 = along_z(own, -1)
    near = jnp.stack([own, below1, above1, below2, above2])
    below3 = along_z(below2, 1)
    above3 = along_z(above2, -1)
    far_low = along_z(below2[:, :half], 2)
    far_high = along_z(above2[:, half:], -2)
    far = jnp.stack([below3, above3, jnp.concatenate([far_low, far_high], axis=1)])
    return near, far


def sum_column(parts):
    own, above1, below1, above2, below2, above3, below3, far = [
        parts[step] for step in (0, 2, 1, 4, 3, 6, 5, 7)
    ]
    half = own.shape[1] // 256 * 128
    got_up = along_z(jnp.stack([above1, above3]).astype(jnp.bfloat16), 1)
    got_down = along_z(jnp.stack([below1, below3]).astype(jnp.bfloat16), -1)
    far = far.astype(jnp.bfloat16)
    far_low = along_z(far[:, :half], 2).astype(jnp.float32)
    far_high = along_z(far[:, half:], -2).astype(jnp.float32)
    above2 = above2 + got_up[1].astype(jnp.float32)
    below2 = below2 + got_down[1].astype(jnp.float32)
    above2 = jnp.concatenate([above2[:, :half] + far_low, above2[:, half:]], axis=1)
    below2 = jnp.concatenate([below2[:, :half], below2[:, half:] + far_high], axis=1)
    two_up = along_z(above2.astype(jnp.bfloat16), 2)
    two_down = along_z(below2.astype(jnp.bfloat16), -2)
    near = own + got_up[0].astype(jnp.float32) + got_down[0].astype(jnp.float32)
    return near + two_up.astype(jnp.float32) + two_down.astype(jnp.float32)


def body(
    fwd_in,
    fwd_ids,
    fwd_lengths,
    bwd_in,
    bwd_grad,
    bwd_ids,
    bwd_lengths,
    norm_gain,
    router,
    w_gate,
    w_up,
    w_down,
):
    tok_count, width = fwd_in.shape[1:]
    capacity = max(2, 2 * tok_count // EXPERTS)
    n_dp = lax.axis_size("dp")
    norm_w = norm_gain[0]
    router_w = router[0]
    gate_w = w_gate[0]
    up_w = w_up[0]
    down_w = w_down[0]
    positions = jnp.arange(tok_count, dtype=jnp.int32)

    def hidden_parts(slot_rows):
        gate_pre = jnp.dot(slot_rows, gate_w, preferred_element_type=jnp.float32)
        up_pre = jnp.dot(slot_rows, up_w, preferred_element_type=jnp.float32)
        hidden = (gate_pre * jax.nn.sigmoid(gate_pre) * up_pre).astype(jnp.bfloat16)
        return (gate_pre, up_pre, hidden)

    def slot_side(tokens, ids, length):
        placing = placement_matrix(slot_of(ids, capacity), capacity)
        mask = (positions < length).astype(jnp.float32)
        slot_mask = jnp.sum(placing.astype(jnp.float32) * mask[None, :], axis=1)
        values = pack_rows(placing, tokens)
        inv, normed = normalize(values, norm_w)
        logit = jnp.dot(normed, router_w, preferred_element_type=jnp.float32)
        return placing, slot_mask, values, inv, normed, jax.nn.sigmoid(logit)

    next_tokens = shifted(fwd_in[0], "pipe", 1)
    prev_grads = shifted(bwd_grad[0], "pipe", -1)

    b_place, b_mask, b_values, b_inv, b_normed, b_prob = slot_side(
        bwd_in[0], bwd_ids[0], bwd_lengths[0, 0]
    )
    g_values = pack_rows(b_place, bwd_grad[0])
    g_send = (g_values * b_mask[:, None]).astype(jnp.bfloat16)
    f_place, f_mask, f_values, f_inv, f_normed, f_prob = slot_side(
        fwd_in[0], fwd_ids[0], fwd_lengths[0, 0]
    )

    near, far = gather_column(jnp.concatenate([b_normed, g_send, f_normed], axis=0))
    rows = jnp.concatenate([near, far, swap_x(near), swap_x(far)], axis=0)
    b_rows, g_rows, f_rows = [
        rows[:, part * capacity : (part + 1) * capacity].reshape(n_dp * capacity, width)
        for part in range(3)
    ]
    column = n_dp // 2

    gate_pre, up_pre, hidden = hidden_parts(b_rows)
    d_hidden = lax.dot_general(
        g_rows, down_w, (((1,), (1,)), ((), ())), preferred_element_type=jnp.float32
    )
    dot_part = jnp.sum(hidden.astype(jnp.float32) * d_hidden, axis=1)
    gate_sig = jax.nn.sigmoid(gate_pre)
    d_gate = (d_hidden * up_pre * gate_sig * (1.0 + gate_pre * (1.0 - gate_sig))).astype(
        jnp.bfloat16
    )
    d_up = (d_hidden * gate_pre * gate_sig).astype(jnp.bfloat16)
    d_part = lax.dot_general(
        d_gate, gate_w, (((1,), (1,)), ((), ())), preferred_element_type=jnp.float32
    )
    d_part = d_part + lax.dot_general(
        d_up, up_w, (((1,), (1,)), ((), ())), preferred_element_type=jnp.float32
    )
    dot_high = dot_part.astype(jnp.bfloat16)
    dot_low = (dot_part - dot_high.astype(jnp.float32)).astype(jnp.bfloat16)
    lanes = jnp.arange(128)[None, :]
    dot_cols = jnp.where(
        lanes == 0, dot_high[:, None], jnp.where(lanes == 1, dot_low[:, None], 0)
    ).astype(jnp.bfloat16)
    d_parts = jnp.concatenate([d_part.astype(jnp.bfloat16), dot_cols], axis=1)
    d_parts = d_parts.reshape(2, column, capacity, width + 128)
    d_parts = d_parts[0].astype(jnp.float32) + swap_x(d_parts[1]).astype(jnp.float32)

    f_hidden = hidden_parts(f_rows)[2]
    f_parts = jnp.dot(f_hidden, down_w, preferred_element_type=jnp.float32).astype(jnp.bfloat16)
    f_parts = f_parts.reshape(2, column, capacity, width)
    f_parts = f_parts[0].astype(jnp.float32) + swap_x(f_parts[1]).astype(jnp.float32)

    both = sum_column(jnp.concatenate([d_parts, f_parts], axis=2))
    d_sum = both[:, : width + 128]
    f_back = both[:, width + 128 :].astype(jnp.bfloat16)

    def with_place(rows, placing):
        return jnp.concatenate(
            [rows, jnp.pad(placing, ((0, 0), (0, 128 - tok_count)))], axis=1
        )

    d_rows = d_sum[:, :width].astype(jnp.bfloat16).astype(jnp.float32)
    row_dot = d_sum[:, width] + d_sum[:, width + 1]
    d_logit = b_mask * row_dot * b_prob * (1.0 - b_prob)
    d_normed = b_prob[:, None] * d_rows + d_logit[:, None] * router_w.astype(jnp.float32)[None, :]
    weighted = norm_w * d_normed
    inner = jnp.mean(weighted * b_values, axis=-1, keepdims=True)
    d_input = (g_values + b_inv * weighted - b_values * b_inv * b_inv * b_inv * inner).astype(
        jnp.bfloat16
    )
    d_moved = shifted(with_place(d_input, b_place), "pipe", -1)
    layer_rows = (f_values + (f_mask * f_prob)[:, None] * f_back.astype(jnp.float32)).astype(
        jnp.bfloat16
    )
    f_moved = shifted(with_place(layer_rows, f_place), "pipe", 1)

    def finished(moved, tokens):
        return overlay(moved[:, width : width + tok_count], moved[:, :width], tokens)

    return (finished(f_moved, next_tokens)[None], finished(d_moved, prev_grads)[None])


def solution(mesh):
    in_specs = (
        P("pipe", "dp", None),
        P("pipe", "dp"),
        P("pipe", "dp"),
        P("pipe", "dp", None),
        P("pipe", "dp", None),
        P("pipe", "dp"),
        P("pipe", "dp"),
        P("pipe", None),
        P("pipe", None),
        P("pipe", None, "dp"),
        P("pipe", None, "dp"),
        P("pipe", "dp", None),
    )
    out_specs = (P("pipe", "dp", None), P("pipe", "dp", None))
    return jax.shard_map(body, mesh=mesh, in_specs=in_specs, out_specs=out_specs, check_vma=False)
```

```python
import jax
import jax.numpy as jnp
from jax import lax
from jax.experimental import pallas as pl
from jax.experimental.pallas import tpu as pltpu
from jax.sharding import PartitionSpec as P

EXPERTS = 16
EPS = 1e-05
LANES = 128
CHUNKS = 3
VMEM_LIMIT = 20 * 1024 * 1024
VMEM = pl.BlockSpec(memory_space=pltpu.VMEM)
SMEM = pl.BlockSpec(memory_space=pltpu.SMEM)
NT = (((1,), (1,)), ((), ()))
TN = (((0,), (0,)), ((), ()))


def along_z(value, steps):
    count = lax.axis_size("dp")
    pairs = [(source, (source + 2 * steps) % count) for source in range(count)]
    return lax.ppermute(value, "dp", pairs)


def swap_x(value):
    count = lax.axis_size("dp")
    return lax.ppermute(value, "dp", [(source, source ^ 1) for source in range(count)])


def across(value, stages, steps):
    n_pipe, n_dp = lax.axis_size("pipe"), lax.axis_size("dp")
    pairs = [
        (p * n_dp + d, (p + stages) % n_pipe * n_dp + (d + 2 * steps) % n_dp)
        for p in range(n_pipe)
        for d in range(n_dp)
    ]
    return lax.ppermute(value, ("pipe", "dp"), pairs)


def split3(value):
    high = value.astype(jnp.bfloat16)
    rest = value - high.astype(jnp.float32)
    middle = rest.astype(jnp.bfloat16)
    low = (rest - middle.astype(jnp.float32)).astype(jnp.bfloat16)
    return [part.astype(jnp.float32) for part in (high, middle, low)]


def columns(parts, rows):
    lane = lax.broadcasted_iota(jnp.int32, (rows, LANES), 1)
    out = jnp.zeros((rows, LANES), jnp.float32)
    for at, part in parts:
        out = jnp.where(lane == at, part, out)
    return out


def head_kernel(capacity, f_ids, b_ids, f_len, b_len, f_in, b_in, grad, gain, router, rows, f_pack, b_pack):
    tok_count = f_in.shape[0]

    def place(ids):
        chosen = jnp.where(ids[...] == 0, 1.0, 0.0)
        chosen = jnp.broadcast_to(chosen, (capacity, tok_count))
        before = lax.broadcasted_iota(jnp.int32, (tok_count, tok_count), 0)
        after = lax.broadcasted_iota(jnp.int32, (tok_count, tok_count), 1)
        upto = jnp.where(before <= after, 1.0, 0.0).astype(jnp.bfloat16)
        rank = jnp.dot(chosen.astype(jnp.bfloat16), upto, preferred_element_type=jnp.float32)
        slot = lax.broadcasted_iota(jnp.int32, (capacity, tok_count), 0).astype(jnp.float32)
        return jnp.where((rank - 1.0 == slot) & (chosen > 0.0), 1.0, 0.0)

    def side(ids, length, tokens):
        placing = place(ids)
        position = lax.broadcasted_iota(jnp.int32, (capacity, tok_count), 1)
        mask = jnp.sum(jnp.where(position < length[0, 0], placing, 0.0), axis=1, keepdims=True)
        values = jnp.dot(
            placing.astype(jnp.bfloat16), tokens[...], preferred_element_type=jnp.float32
        )
        inv = lax.rsqrt(jnp.mean(values * values, axis=1, keepdims=True) + EPS)
        normed = (values * inv * gain[...]).astype(jnp.bfloat16).astype(jnp.float32)
        logit = jnp.sum(normed * router[...].astype(jnp.float32), axis=1, keepdims=True)
        prob = 1.0 / (1.0 + jnp.exp(-logit))
        return placing, mask, values, inv, normed, prob

    def lanes_of(placing, scalars):
        parts = []
        for at, scalar in enumerate(scalars):
            parts += [(tok_count + 3 * at + i, part) for i, part in enumerate(split3(scalar))]
        wide = jnp.concatenate([placing, jnp.zeros((capacity, LANES - tok_count), jnp.float32)], axis=1)
        return wide + columns(parts, capacity)

    placing, mask, values, inv, normed, prob = side(b_ids, b_len, b_in)
    grads = jnp.dot(placing.astype(jnp.bfloat16), grad[...], preferred_element_type=jnp.float32)
    gain_parts = split3(gain[...])
    router32 = router[...].astype(jnp.float32)
    width = values.shape[1]
    meta = jnp.concatenate([values] + gain_parts + [router32, jnp.zeros((4, width), jnp.float32)], axis=0)
    b_lanes = lanes_of(placing, (prob, inv, mask * prob * (1.0 - prob)))
    b_pack[:tok_count, :width] = grad[...]
    b_pack[tok_count:, :width] = meta.astype(jnp.bfloat16)
    b_pack[:tok_count, width:] = jnp.zeros((tok_count, LANES), jnp.bfloat16)
    b_pack[tok_count:, width:] = jnp.concatenate([b_lanes, jnp.zeros_like(b_lanes)], axis=0).astype(jnp.bfloat16)
    f_placing, f_mask, f_values, f_inv, f_normed, f_prob = side(f_ids, f_len, f_in)
    rows[...] = jnp.concatenate([normed, grads * mask, f_normed], axis=0).astype(jnp.bfloat16)
    f_lanes = lanes_of(f_placing, (f_mask * f_prob,))
    f_pack[:, :width] = f_in[...]
    f_pack[:, width:] = jnp.concatenate(
        [f_lanes, jnp.zeros((tok_count - capacity, LANES), jnp.float32)], axis=0
    ).astype(jnp.bfloat16)


def head(capacity, f_ids, b_ids, f_len, b_len, f_in, b_in, grad, gain, router):
    tok_count, width = f_in.shape
    return pl.pallas_call(
        lambda *refs: head_kernel(capacity, *refs),
        out_shape=(
            jax.ShapeDtypeStruct((3 * capacity, width), jnp.bfloat16),
            jax.ShapeDtypeStruct((tok_count, width + LANES), jnp.bfloat16),
            jax.ShapeDtypeStruct((tok_count + 2 * capacity, width + LANES), jnp.bfloat16),
        ),
        in_specs=[VMEM, VMEM, SMEM, SMEM] + [VMEM] * 5,
        out_specs=(VMEM,) * 3,
        compiler_params=pltpu.CompilerParams(vmem_limit_bytes=8 * 1024 * 1024),
        name="head",
    )(f_ids, b_ids, f_len, b_len, f_in, b_in, grad, gain, router)


def sigmoid(value):
    return 1.0 / (1.0 + jnp.exp(-value))


def dot_t(left, right):
    return lax.dot_general(left, right, NT, preferred_element_type=jnp.float32)


def dot(left, right):
    return jnp.dot(left, right, preferred_element_type=jnp.float32)


def chunk_of(step, weights):
    part = weights[0].shape[0] // CHUNKS
    return [weight[step * part : (step + 1) * part] for weight in weights]


def forward_kernel(own, other, after, gate_w, up_w, down_w, mine, theirs, rows, total):
    half = own.shape[0]
    rows[:half] = own[...]
    rows[half:] = other[...]
    for step in range(CHUNKS):
        gate, up, down = chunk_of(step, (gate_w, up_w, down_w))
        gate_pre = dot_t(rows[...], gate)
        up_pre = dot_t(rows[...], up)
        hidden = (gate_pre * sigmoid(gate_pre) * up_pre).astype(jnp.bfloat16)
        if step == 0:
            total[...] = dot(hidden, down)
        elif step < CHUNKS - 1:
            total[...] += dot(hidden, down)
        else:
            part = total[...] + dot(hidden, down)
            mine[...] = part[:half]
            theirs[...] = part[half:].astype(jnp.bfloat16)


def backward_kernel(capacity, groups, after, gate_w, up_w, down_w, mine, theirs, rows, grads, total):
    half, width = mine.shape[0], rows.shape[1]
    pair = 2 * capacity
    blocks = [(ref, at) for ref in groups for at in range(0, ref.shape[0], pair)]
    for at in range(0, len(blocks), 2):
        low, high = [ref[start : start + pair].astype(jnp.float32) for ref, start in blocks[at : at + 2]]
        place = slice(at * capacity, at * capacity + pair)
        rows[place] = jnp.concatenate([low[:capacity], high[:capacity]], axis=0).astype(jnp.bfloat16)
        grads[place] = jnp.concatenate([low[capacity:], high[capacity:]], axis=0).astype(jnp.bfloat16)

    dots = jnp.zeros((2 * half, 1), jnp.float32)
    for step in range(CHUNKS):
        gate, up, down = chunk_of(step, (gate_w, up_w, down_w))
        gate_pre = dot_t(rows[...], gate)
        up_pre = dot_t(rows[...], up)
        d_hidden = dot_t(grads[...], down)
        gate_sig = sigmoid(gate_pre)
        silu = gate_pre * gate_sig
        hidden = (silu * up_pre).astype(jnp.bfloat16).astype(jnp.float32)
        dots += jnp.sum(hidden * d_hidden, axis=1, keepdims=True)
        d_gate = (d_hidden * up_pre * gate_sig * (1.0 + gate_pre * (1.0 - gate_sig))).astype(jnp.bfloat16)
        d_up = (d_hidden * silu).astype(jnp.bfloat16)
        part = dot(d_gate, gate) + dot(d_up, up)
        if step == 0:
            total[...] = part
        elif step < CHUNKS - 1:
            total[...] += part
        else:
            part += total[...]
            mine[:, :width] = part[:half]
            theirs[:, :width] = part[half:].astype(jnp.bfloat16)
    high = dots.astype(jnp.bfloat16).astype(jnp.float32)
    tail = columns([(0, high), (1, dots - high)], 2 * half)
    mine[:, width:] = tail[:half]
    theirs[:, width:] = tail[half:].astype(jnp.bfloat16)


def expert_call(kernel, name, operands, weights, extra, count, spaces, products, scratch):
    hidden, width = weights[0].shape
    half = count // 2
    return pl.pallas_call(
        kernel,
        out_shape=(
            jax.ShapeDtypeStruct((half, width + extra), jnp.float32),
            jax.ShapeDtypeStruct((half, width + extra), jnp.bfloat16),
        ),
        in_specs=spaces + [VMEM] * 3,
        out_specs=(VMEM, VMEM),
        scratch_shapes=[pltpu.VMEM((count, width), jnp.bfloat16)] * scratch
        + [pltpu.VMEM((count, width), jnp.float32)],
        compiler_params=pltpu.CompilerParams(vmem_limit_bytes=VMEM_LIMIT),
        cost_estimate=pl.CostEstimate(
            flops=products * 2 * count * hidden * width, bytes_accessed=6 * hidden * width, transcendentals=0
        ),
        name=name,
    )(*operands, *weights)


def hold(after, weights):
    def kernel(after, gate_w, up_w, down_w, held):
        held[...] = jnp.zeros_like(held)

    return pl.pallas_call(
        kernel,
        out_shape=jax.ShapeDtypeStruct((8, LANES), jnp.float32),
        in_specs=[pl.BlockSpec(memory_space=pl.ANY)] + [VMEM] * 3,
        out_specs=VMEM,
        compiler_params=pltpu.CompilerParams(vmem_limit_bytes=2 * 1024 * 1024),
        cost_estimate=pl.CostEstimate(
            flops=0, bytes_accessed=6 * weights[0].shape[0] * weights[0].shape[1], transcendentals=0
        ),
        name="hold",
    )(after, *weights)


def forward_expert(own, other, after, weights):
    spaces = [VMEM, VMEM, pl.BlockSpec(memory_space=pl.ANY)]
    return expert_call(
        forward_kernel, "forward_expert", (own, other, after), weights, 0, 2 * own.shape[0], spaces, 3, 1
    )


def backward_expert(capacity, groups, after, weights):
    count = sum(group.shape[0] for group in groups) // 2

    def kernel(*refs):
        backward_kernel(capacity, refs[: len(groups)], *refs[len(groups) :])

    return expert_call(
        kernel,
        "backward_expert",
        groups + [after],
        weights,
        LANES,
        count,
        [VMEM] * len(groups) + [pl.BlockSpec(memory_space=pl.ANY)],
        5,
        2,
    )


def scalar_of(lanes, tok_count, at):
    first = tok_count + 3 * at
    return lanes[:, first : first + 1] + lanes[:, first + 1 : first + 2] + lanes[:, first + 2 : first + 3]


def overlay(placing, rows, tokens, out):
    place16 = placing.astype(jnp.bfloat16)
    placed = lax.dot_general(place16, rows.astype(jnp.bfloat16), TN, preferred_element_type=jnp.float32)
    ones = jnp.ones((placing.shape[0], LANES), jnp.bfloat16)
    chosen = lax.dot_general(place16, ones, TN, preferred_element_type=jnp.float32)
    out[...] = jnp.where(chosen[:, :1] > 0.0, placed, tokens[...].astype(jnp.float32)).astype(jnp.bfloat16)


def forward_finish_kernel(capacity, sums, pack, out):
    tok_count, width = out.shape
    lanes = pack[:, width:].astype(jnp.float32)[:capacity]
    placing = lanes[:, :tok_count]
    tokens = pack[:, :width]
    values = dot(placing.astype(jnp.bfloat16), tokens)
    result = sums[...].astype(jnp.bfloat16).astype(jnp.float32)
    overlay(placing, values + scalar_of(lanes, tok_count, 0) * result, tokens, out)


def backward_finish_kernel(capacity, sums, pack, out):
    tok_count, width = out.shape
    lanes = pack[tok_count:, width:].astype(jnp.float32)[:capacity]
    wide = pack[tok_count:, :width].astype(jnp.float32)
    tokens = pack[:tok_count, :width]
    values = wide[:capacity]
    gain = wide[capacity : capacity + 1] + wide[capacity + 1 : capacity + 2] + wide[capacity + 2 : capacity + 3]
    router = wide[capacity + 3 : capacity + 4]
    placing = lanes[:, :tok_count]
    prob, inv, slope = [scalar_of(lanes, tok_count, at) for at in range(3)]
    grads = dot(placing.astype(jnp.bfloat16), tokens)
    d_rows = sums[:, :width].astype(jnp.bfloat16).astype(jnp.float32)
    row_dot = sums[:, width : width + 1] + sums[:, width + 1 : width + 2]
    weighted = gain * (prob * d_rows + (slope * row_dot) * router)
    inner = jnp.mean(weighted * values, axis=1, keepdims=True)
    overlay(placing, grads + inv * weighted - values * inv * inv * inv * inner, tokens, out)


def finish(kernel, name, capacity, sums, pack, tok_count):
    return pl.pallas_call(
        lambda *refs: kernel(capacity, *refs),
        out_shape=jax.ShapeDtypeStruct((tok_count, pack.shape[1] - LANES), pack.dtype),
        in_specs=[VMEM, VMEM],
        out_specs=VMEM,
        compiler_params=pltpu.CompilerParams(vmem_limit_bytes=8 * 1024 * 1024),
        name=name,
    )(sums, pack)


def gather_column(own):
    half = own.shape[1] // (2 * LANES) * LANES
    below2 = along_z(own, 2)
    above2 = along_z(own, -2)
    below1 = along_z(own, 1)
    above1 = along_z(own, -1)
    below3 = along_z(below2, 1)
    above3 = along_z(above2, -1)
    far_low = along_z(below2[:, :half], 2)
    far_high = along_z(above2[:, half:], -2)
    far = jnp.concatenate([far_low, far_high], axis=1)
    return [own], [below1, above1, below2, above2], [below3, above3, far]


def sum_columns(b_total, f_total, capacity):
    width = b_total.shape[1]
    low, full = jnp.bfloat16, jnp.float32
    total = jnp.concatenate([b_total, f_total], axis=1)
    own, below1, above1, below2, above2, below3, above3, far = [
        total[at * capacity : (at + 1) * capacity] for at in range(total.shape[0] // capacity)
    ]
    up = along_z(jnp.concatenate([above1, above3], axis=0).astype(low), 1).astype(full)
    down = along_z(jnp.concatenate([below1, below3], axis=0).astype(low), -1).astype(full)
    far_b = along_z(far[:, :width].astype(low), 2).astype(full)
    far_f = along_z(far[:, width:].astype(low), -2).astype(full)
    above2 = above2 + up[capacity:]
    below2 = below2 + down[capacity:]
    near = own + up[:capacity] + down[:capacity]
    b_up = across((above2[:, :width] + far_b).astype(low), -1, 2)
    b_down = across(below2[:, :width].astype(low), -1, -2)
    f_up = across(above2[:, width:].astype(low), 1, 2)
    f_down = across((below2[:, width:] + far_f).astype(low), 1, -2)
    b_near = across(near[:, :width].astype(low), -1, 0)
    f_near = across(near[:, width:].astype(low), 1, 0)

    def add(parts):
        return sum(part.astype(full) for part in parts)

    return add((b_near, b_up, b_down)), add((f_near, f_up, f_down))


def body(
    fwd_in,
    fwd_ids,
    fwd_lengths,
    bwd_in,
    bwd_grad,
    bwd_ids,
    bwd_lengths,
    norm_gain,
    router,
    w_gate,
    w_up,
    w_down,
):
    tok_count = fwd_in.shape[1]
    capacity = max(2, 2 * tok_count // EXPERTS)
    weights = (w_gate[0].T, w_up[0].T, w_down[0])

    rows, f_pack, b_pack = head(
        capacity, fwd_ids, bwd_ids, fwd_lengths, bwd_lengths, fwd_in[0], bwd_in[0], bwd_grad[0], norm_gain, router
    )
    f_pack = across(f_pack, 1, 0)
    b_pack = across(b_pack, -1, 0)
    own, near, far = gather_column(rows)
    pair = 2 * capacity
    groups = [jnp.concatenate([block[:pair] for block in group], axis=0) for group in (own, near, far)]
    f_own = jnp.concatenate([block[pair:] for block in own + near + far], axis=0)
    others = [swap_x(group) for group in groups]
    f_own, others[2] = lax.optimization_barrier((f_own, others[2]))
    f_other = swap_x(f_own)

    b_mine, b_theirs = backward_expert(capacity, groups + others, hold(groups[2], weights), weights)
    f_mine, f_theirs = forward_expert(f_own, f_other, b_theirs, weights)
    b_total = b_mine + swap_x(b_theirs).astype(jnp.float32)
    f_total = f_mine + swap_x(f_theirs).astype(jnp.float32)
    b_sums, f_sums = sum_columns(b_total, f_total, capacity)
    bwd_out = finish(backward_finish_kernel, "backward_finish", capacity, b_sums, b_pack, tok_count)
    fwd_out = finish(forward_finish_kernel, "forward_finish", capacity, f_sums, f_pack, tok_count)
    return (fwd_out[None], bwd_out[None])


def solution(mesh):
    in_specs = (
        P("pipe", "dp", None),
        P("pipe", "dp"),
        P("pipe", "dp"),
        P("pipe", "dp", None),
        P("pipe", "dp", None),
        P("pipe", "dp"),
        P("pipe", "dp"),
        P("pipe", None),
        P("pipe", None),
        P("pipe", None, "dp"),
        P("pipe", None, "dp"),
        P("pipe", "dp", None),
    )
    out_specs = (P("pipe", "dp", None), P("pipe", "dp", None))
    return jax.shard_map(body, mesh=mesh, in_specs=in_specs, out_specs=out_specs, check_vma=False)
```

```python
import jax
import jax.numpy as jnp
from jax import lax
from jax.experimental import pallas as pl
from jax.experimental.pallas import tpu as pltpu
from jax.sharding import PartitionSpec as P

EXPERTS = 16
EPS = 1e-05
LANES = 128
CHUNKS = 3
VMEM_LIMIT = 20 * 1024 * 1024
VMEM = pl.BlockSpec(memory_space=pltpu.VMEM)
SMEM = pl.BlockSpec(memory_space=pltpu.SMEM)
NT = (((1,), (1,)), ((), ()))
TN = (((0,), (0,)), ((), ()))


def along_z(value, steps):
    count = lax.axis_size("dp")
    pairs = [(source, (source + 2 * steps) % count) for source in range(count)]
    return lax.ppermute(value, "dp", pairs)


def swap_x(value):
    count = lax.axis_size("dp")
    return lax.ppermute(value, "dp", [(source, source ^ 1) for source in range(count)])


def across(value, stages, steps):
    n_pipe, n_dp = lax.axis_size("pipe"), lax.axis_size("dp")
    pairs = [
        (p * n_dp + d, (p + stages) % n_pipe * n_dp + (d + 2 * steps) % n_dp)
        for p in range(n_pipe)
        for d in range(n_dp)
    ]
    return lax.ppermute(value, ("pipe", "dp"), pairs)


def split3(value):
    high = value.astype(jnp.bfloat16)
    rest = value - high.astype(jnp.float32)
    middle = rest.astype(jnp.bfloat16)
    low = (rest - middle.astype(jnp.float32)).astype(jnp.bfloat16)
    return [part.astype(jnp.float32) for part in (high, middle, low)]


def columns(parts, rows):
    lane = lax.broadcasted_iota(jnp.int32, (rows, LANES), 1)
    out = jnp.zeros((rows, LANES), jnp.float32)
    for at, part in parts:
        out = jnp.where(lane == at, part, out)
    return out


def head_kernel(capacity, f_ids, b_ids, f_len, b_len, f_in, b_in, grad, gain, router, rows, f_pack, b_pack):
    tok_count = f_in.shape[0]

    def place(ids):
        chosen = jnp.where(ids[...] == 0, 1.0, 0.0)
        chosen = jnp.broadcast_to(chosen, (capacity, tok_count))
        before = lax.broadcasted_iota(jnp.int32, (tok_count, tok_count), 0)
        after = lax.broadcasted_iota(jnp.int32, (tok_count, tok_count), 1)
        upto = jnp.where(before <= after, 1.0, 0.0).astype(jnp.bfloat16)
        rank = jnp.dot(chosen.astype(jnp.bfloat16), upto, preferred_element_type=jnp.float32)
        slot = lax.broadcasted_iota(jnp.int32, (capacity, tok_count), 0).astype(jnp.float32)
        return jnp.where((rank - 1.0 == slot) & (chosen > 0.0), 1.0, 0.0)

    def side(ids, length, tokens):
        placing = place(ids)
        position = lax.broadcasted_iota(jnp.int32, (capacity, tok_count), 1)
        mask = jnp.sum(jnp.where(position < length[0, 0], placing, 0.0), axis=1, keepdims=True)
        values = jnp.dot(
            placing.astype(jnp.bfloat16), tokens[...], preferred_element_type=jnp.float32
        )
        inv = lax.rsqrt(jnp.mean(values * values, axis=1, keepdims=True) + EPS)
        normed = (values * inv * gain[...]).astype(jnp.bfloat16).astype(jnp.float32)
        logit = jnp.sum(normed * router[...].astype(jnp.float32), axis=1, keepdims=True)
        prob = 1.0 / (1.0 + jnp.exp(-logit))
        return placing, mask, values, inv, normed, prob

    def lanes_of(placing, scalars):
        parts = []
        for at, scalar in enumerate(scalars):
            parts += [(tok_count + 3 * at + i, part) for i, part in enumerate(split3(scalar))]
        wide = jnp.concatenate([placing, jnp.zeros((capacity, LANES - tok_count), jnp.float32)], axis=1)
        return wide + columns(parts, capacity)

    placing, mask, values, inv, normed, prob = side(b_ids, b_len, b_in)
    grads = jnp.dot(placing.astype(jnp.bfloat16), grad[...], preferred_element_type=jnp.float32)
    gain_parts = split3(gain[...])
    router32 = router[...].astype(jnp.float32)
    width = values.shape[1]
    meta = jnp.concatenate([values] + gain_parts + [router32, jnp.zeros((4, width), jnp.float32)], axis=0)
    b_lanes = lanes_of(placing, (prob, inv, mask * prob * (1.0 - prob)))
    b_pack[:tok_count, :width] = grad[...]
    b_pack[tok_count:, :width] = meta.astype(jnp.bfloat16)
    b_pack[:tok_count, width:] = jnp.zeros((tok_count, LANES), jnp.bfloat16)
    b_pack[tok_count:, width:] = jnp.concatenate([b_lanes, jnp.zeros_like(b_lanes)], axis=0).astype(jnp.bfloat16)
    f_placing, f_mask, f_values, f_inv, f_normed, f_prob = side(f_ids, f_len, f_in)
    rows[...] = jnp.concatenate([normed, grads * mask, f_normed], axis=0).astype(jnp.bfloat16)
    f_lanes = lanes_of(f_placing, (f_mask * f_prob,))
    f_pack[:, :width] = f_in[...]
    f_pack[:, width:] = jnp.concatenate(
        [f_lanes, jnp.zeros((tok_count - capacity, LANES), jnp.float32)], axis=0
    ).astype(jnp.bfloat16)


def fetched_head_kernel(capacity, f_len, b_len, *refs):
    count = 7
    sources, outs, held, arrived = refs[:count], refs[count : count + 3], refs[count + 3 : -1], refs[-1]
    copies = [
        pltpu.make_async_copy(source, target, arrived.at[at])
        for at, (source, target) in enumerate(zip(sources, held))
    ]
    for copy in copies:
        copy.start()
    for copy in copies:
        copy.wait()
    f_ids, b_ids, *tokens = held
    head_kernel(capacity, f_ids, b_ids, f_len, b_len, *tokens, *outs)


def head(capacity, f_ids, b_ids, f_len, b_len, f_in, b_in, grad, gain, router):
    tok_count, width = f_in.shape
    sources = (f_ids, b_ids, f_in, b_in, grad, gain, router)
    return pl.pallas_call(
        lambda *refs: fetched_head_kernel(capacity, *refs),
        out_shape=(
            jax.ShapeDtypeStruct((3 * capacity, width), jnp.bfloat16),
            jax.ShapeDtypeStruct((tok_count, width + LANES), jnp.bfloat16),
            jax.ShapeDtypeStruct((tok_count + 2 * capacity, width + LANES), jnp.bfloat16),
        ),
        in_specs=[SMEM, SMEM] + [pl.BlockSpec(memory_space=pl.ANY)] * len(sources),
        out_specs=(VMEM,) * 3,
        scratch_shapes=[pltpu.VMEM(source.shape, source.dtype) for source in sources]
        + [pltpu.SemaphoreType.DMA((len(sources),))],
        compiler_params=pltpu.CompilerParams(vmem_limit_bytes=56 * 1024 * 1024),
        name="head",
    )(f_len, b_len, *sources)


def sigmoid(value):
    return 1.0 / (1.0 + jnp.exp(-value))


def dot_t(left, right):
    return lax.dot_general(left, right, NT, preferred_element_type=jnp.float32)


def dot(left, right):
    return jnp.dot(left, right, preferred_element_type=jnp.float32)


def chunk_of(step, weights):
    part = weights[0].shape[0] // CHUNKS
    return [weight[step * part : (step + 1) * part] for weight in weights]


def forward_kernel(own, other, after, gate_w, up_w, down_w, mine, theirs, rows, total):
    half = own.shape[0]
    rows[:half] = own[...]
    rows[half:] = other[...]
    for step in range(CHUNKS):
        gate, up, down = chunk_of(step, (gate_w, up_w, down_w))
        gate_pre = dot_t(rows[...], gate)
        up_pre = dot_t(rows[...], up)
        hidden = (gate_pre * sigmoid(gate_pre) * up_pre).astype(jnp.bfloat16)
        if step == 0:
            total[...] = dot(hidden, down)
        elif step < CHUNKS - 1:
            total[...] += dot(hidden, down)
        else:
            part = total[...] + dot(hidden, down)
            mine[...] = part[:half]
            theirs[...] = part[half:].astype(jnp.bfloat16)


def backward_kernel(capacity, groups, after, gate_w, up_w, down_w, mine, theirs, rows, grads, total):
    half, width = mine.shape[0], rows.shape[1]
    pair = 2 * capacity
    blocks = [(ref, at) for ref in groups for at in range(0, ref.shape[0], pair)]
    for at in range(0, len(blocks), 2):
        low, high = [ref[start : start + pair].astype(jnp.float32) for ref, start in blocks[at : at + 2]]
        place = slice(at * capacity, at * capacity + pair)
        rows[place] = jnp.concatenate([low[:capacity], high[:capacity]], axis=0).astype(jnp.bfloat16)
        grads[place] = jnp.concatenate([low[capacity:], high[capacity:]], axis=0).astype(jnp.bfloat16)

    dots = jnp.zeros((2 * half, 1), jnp.float32)
    for step in range(CHUNKS):
        gate, up, down = chunk_of(step, (gate_w, up_w, down_w))
        gate_pre = dot_t(rows[...], gate)
        up_pre = dot_t(rows[...], up)
        d_hidden = dot_t(grads[...], down)
        gate_sig = sigmoid(gate_pre)
        silu = gate_pre * gate_sig
        hidden = (silu * up_pre).astype(jnp.bfloat16).astype(jnp.float32)
        dots += jnp.sum(hidden * d_hidden, axis=1, keepdims=True)
        d_gate = (d_hidden * up_pre * gate_sig * (1.0 + gate_pre * (1.0 - gate_sig))).astype(jnp.bfloat16)
        d_up = (d_hidden * silu).astype(jnp.bfloat16)
        part = dot(d_gate, gate) + dot(d_up, up)
        if step == 0:
            total[...] = part
        elif step < CHUNKS - 1:
            total[...] += part
        else:
            part += total[...]
            mine[:, :width] = part[:half]
            theirs[:, :width] = part[half:].astype(jnp.bfloat16)
    high = dots.astype(jnp.bfloat16).astype(jnp.float32)
    tail = columns([(0, high), (1, dots - high)], 2 * half)
    mine[:, width:] = tail[:half]
    theirs[:, width:] = tail[half:].astype(jnp.bfloat16)


def expert_call(kernel, name, operands, weights, extra, count, spaces, products, scratch):
    hidden, width = weights[0].shape
    half = count // 2
    return pl.pallas_call(
        kernel,
        out_shape=(
            jax.ShapeDtypeStruct((half, width + extra), jnp.float32),
            jax.ShapeDtypeStruct((half, width + extra), jnp.bfloat16),
        ),
        in_specs=spaces + [VMEM] * 3,
        out_specs=(VMEM, VMEM),
        scratch_shapes=[pltpu.VMEM((count, width), jnp.bfloat16)] * scratch
        + [pltpu.VMEM((count, width), jnp.float32)],
        compiler_params=pltpu.CompilerParams(vmem_limit_bytes=VMEM_LIMIT),
        cost_estimate=pl.CostEstimate(
            flops=products * 2 * count * hidden * width, bytes_accessed=6 * hidden * width, transcendentals=0
        ),
        name=name,
    )(*operands, *weights)


def hold(after, weights):
    def kernel(*refs):
        held = refs[-1]
        held[...] = jnp.zeros_like(held)

    return pl.pallas_call(
        kernel,
        out_shape=jax.ShapeDtypeStruct((8, LANES), jnp.float32),
        in_specs=[pl.BlockSpec(memory_space=pl.ANY)] * len(after) + [VMEM] * 3,
        out_specs=VMEM,
        compiler_params=pltpu.CompilerParams(vmem_limit_bytes=2 * 1024 * 1024),
        cost_estimate=pl.CostEstimate(
            flops=0, bytes_accessed=6 * weights[0].shape[0] * weights[0].shape[1], transcendentals=0
        ),
        name="hold",
    )(*after, *weights)


def forward_expert(own, other, after, weights):
    spaces = [VMEM, VMEM, pl.BlockSpec(memory_space=pl.ANY)]
    return expert_call(
        forward_kernel, "forward_expert", (own, other, after), weights, 0, 2 * own.shape[0], spaces, 3, 1
    )


def backward_expert(capacity, groups, after, weights):
    count = sum(group.shape[0] for group in groups) // 2

    def kernel(*refs):
        backward_kernel(capacity, refs[: len(groups)], *refs[len(groups) :])

    return expert_call(
        kernel,
        "backward_expert",
        groups + [after],
        weights,
        LANES,
        count,
        [VMEM] * len(groups) + [pl.BlockSpec(memory_space=pl.ANY)],
        5,
        2,
    )


def scalar_of(lanes, tok_count, at):
    first = tok_count + 3 * at
    return lanes[:, first : first + 1] + lanes[:, first + 1 : first + 2] + lanes[:, first + 2 : first + 3]


def overlay(placing, rows, tokens, out):
    place16 = placing.astype(jnp.bfloat16)
    placed = lax.dot_general(place16, rows.astype(jnp.bfloat16), TN, preferred_element_type=jnp.float32)
    ones = jnp.ones((placing.shape[0], LANES), jnp.bfloat16)
    chosen = lax.dot_general(place16, ones, TN, preferred_element_type=jnp.float32)
    out[...] = jnp.where(chosen[:, :1] > 0.0, placed, tokens[...].astype(jnp.float32)).astype(jnp.bfloat16)


def forward_finish_kernel(capacity, sums, pack, out):
    tok_count, width = out.shape
    lanes = pack[:, width:].astype(jnp.float32)[:capacity]
    placing = lanes[:, :tok_count]
    tokens = pack[:, :width]
    values = dot(placing.astype(jnp.bfloat16), tokens)
    result = sums[...].astype(jnp.bfloat16).astype(jnp.float32)
    overlay(placing, values + scalar_of(lanes, tok_count, 0) * result, tokens, out)


def backward_finish_kernel(capacity, sums, pack, out):
    tok_count, width = out.shape
    lanes = pack[tok_count:, width:].astype(jnp.float32)[:capacity]
    wide = pack[tok_count:, :width].astype(jnp.float32)
    tokens = pack[:tok_count, :width]
    values = wide[:capacity]
    gain = wide[capacity : capacity + 1] + wide[capacity + 1 : capacity + 2] + wide[capacity + 2 : capacity + 3]
    router = wide[capacity + 3 : capacity + 4]
    placing = lanes[:, :tok_count]
    prob, inv, slope = [scalar_of(lanes, tok_count, at) for at in range(3)]
    grads = dot(placing.astype(jnp.bfloat16), tokens)
    d_rows = sums[:, :width].astype(jnp.bfloat16).astype(jnp.float32)
    row_dot = sums[:, width : width + 1] + sums[:, width + 1 : width + 2]
    weighted = gain * (prob * d_rows + (slope * row_dot) * router)
    inner = jnp.mean(weighted * values, axis=1, keepdims=True)
    overlay(placing, grads + inv * weighted - values * inv * inv * inv * inner, tokens, out)


def finish(kernel, name, capacity, sums, pack, tok_count):
    return pl.pallas_call(
        lambda *refs: kernel(capacity, *refs),
        out_shape=jax.ShapeDtypeStruct((tok_count, pack.shape[1] - LANES), pack.dtype),
        in_specs=[VMEM, VMEM],
        out_specs=VMEM,
        compiler_params=pltpu.CompilerParams(vmem_limit_bytes=8 * 1024 * 1024),
        name=name,
    )(sums, pack)


def gather_column(own):
    half = own.shape[1] // (2 * LANES) * LANES
    below2 = along_z(own, 2)
    above2 = along_z(own, -2)
    below1 = along_z(own, 1)
    above1 = along_z(own, -1)
    below3 = along_z(below2, 1)
    above3 = along_z(above2, -1)
    far_low = along_z(below2[:, :half], 2)
    far_high = along_z(above2[:, half:], -2)
    far = jnp.concatenate([far_low, far_high], axis=1)
    return [own], [below1, above1], [below2, above2], [below3, above3, far]


def sum_columns(b_total, f_total, capacity):
    width = b_total.shape[1]
    low, full = jnp.bfloat16, jnp.float32
    total = jnp.concatenate([b_total, f_total], axis=1)
    own, below1, above1, below2, above2, below3, above3, far = [
        total[at * capacity : (at + 1) * capacity] for at in range(total.shape[0] // capacity)
    ]
    both = total.shape[1]
    up = along_z(jnp.concatenate([above1, below2, far[:, :width]], axis=1).astype(low), 1).astype(full)
    down = along_z(jnp.concatenate([below1, above2, far[:, width:]], axis=1).astype(low), -1).astype(full)
    near = own + up[:, :both] + down[:, :both]
    above3 = above3 + down[:, both : 2 * both]
    below3 = below3 + up[:, both : 2 * both]
    b_up = across((above3[:, :width] + up[:, 2 * both :]).astype(low), -1, 3)
    b_down = across(below3[:, :width].astype(low), -1, -3)
    f_up = across(above3[:, width:].astype(low), 1, 3)
    f_down = across((below3[:, width:] + down[:, 2 * both :]).astype(low), 1, -3)
    b_near = across(near[:, :width].astype(low), -1, 0)
    f_near = across(near[:, width:].astype(low), 1, 0)

    def add(parts):
        return sum(part.astype(full) for part in parts)

    return add((b_near, b_up, b_down)), add((f_near, f_up, f_down))


def body(
    fwd_in,
    fwd_ids,
    fwd_lengths,
    bwd_in,
    bwd_grad,
    bwd_ids,
    bwd_lengths,
    norm_gain,
    router,
    w_gate,
    w_up,
    w_down,
):
    tok_count = fwd_in.shape[1]
    capacity = max(2, 2 * tok_count // EXPERTS)
    weights = (w_gate[0].T, w_up[0].T, w_down[0])

    rows, f_pack, b_pack = head(
        capacity, fwd_ids, bwd_ids, fwd_lengths, bwd_lengths, fwd_in[0], bwd_in[0], bwd_grad[0], norm_gain, router
    )
    f_pack = across(f_pack, 1, 0)
    b_pack = across(b_pack, -1, 0)
    column = gather_column(rows)
    other = swap_x(rows)
    other_near = [along_z(other, 1), along_z(other, -1)]
    pair = 2 * capacity

    def of_backward(blocks):
        return jnp.concatenate([block[:pair] for block in blocks], axis=0)

    def of_forward(blocks):
        return jnp.concatenate([block[pair:] for block in blocks], axis=0)

    own, near, two, far = column
    groups = [of_backward(blocks) for blocks in column]
    others = [of_backward([other]), of_backward(other_near), swap_x(groups[2]), swap_x(groups[3])]
    f_own = of_forward(own + near + two + far)
    loaded = hold((groups[3],), weights)
    f_rest, others[3], loaded = lax.optimization_barrier((of_forward(two + far), others[3], loaded))
    f_other = jnp.concatenate([of_forward([other] + other_near), swap_x(f_rest)], axis=0)

    b_mine, b_theirs = backward_expert(capacity, groups + others, loaded, weights)
    f_mine, f_theirs = forward_expert(f_own, f_other, b_theirs, weights)
    b_total = b_mine + swap_x(b_theirs).astype(jnp.float32)
    f_total = f_mine + swap_x(f_theirs).astype(jnp.float32)
    b_sums, f_sums = sum_columns(b_total, f_total, capacity)
    bwd_out = finish(backward_finish_kernel, "backward_finish", capacity, b_sums, b_pack, tok_count)
    fwd_out = finish(forward_finish_kernel, "forward_finish", capacity, f_sums, f_pack, tok_count)
    return (fwd_out[None], bwd_out[None])


def solution(mesh):
    in_specs = (
        P("pipe", "dp", None),
        P("pipe", "dp"),
        P("pipe", "dp"),
        P("pipe", "dp", None),
        P("pipe", "dp", None),
        P("pipe", "dp"),
        P("pipe", "dp"),
        P("pipe", None),
        P("pipe", None),
        P("pipe", None, "dp"),
        P("pipe", None, "dp"),
        P("pipe", "dp", None),
    )
    out_specs = (P("pipe", "dp", None), P("pipe", "dp", None))
    return jax.shard_map(body, mesh=mesh, in_specs=in_specs, out_specs=out_specs, check_vma=False)
```

```python
import jax
import jax.numpy as jnp
from jax import lax
from jax.experimental import pallas as pl
from jax.experimental.pallas import tpu as pltpu
from jax.sharding import PartitionSpec as P

EXPERTS = 16
EPS = 1e-05
LANES = 128
CHUNKS = 3
VMEM_LIMIT = 20 * 1024 * 1024
VMEM = pl.BlockSpec(memory_space=pltpu.VMEM)
SMEM = pl.BlockSpec(memory_space=pltpu.SMEM)
NT = (((1,), (1,)), ((), ()))
TN = (((0,), (0,)), ((), ()))


def along_z(value, steps):
    count = lax.axis_size("dp")
    pairs = [(source, (source + 2 * steps) % count) for source in range(count)]
    return lax.ppermute(value, "dp", pairs)


def swap_x(value):
    count = lax.axis_size("dp")
    return lax.ppermute(value, "dp", [(source, source ^ 1) for source in range(count)])


def across(value, stages, steps):
    n_pipe, n_dp = lax.axis_size("pipe"), lax.axis_size("dp")
    pairs = [
        (p * n_dp + d, (p + stages) % n_pipe * n_dp + (d + 2 * steps) % n_dp)
        for p in range(n_pipe)
        for d in range(n_dp)
    ]
    return lax.ppermute(value, ("pipe", "dp"), pairs)


def split3(value):
    high = value.astype(jnp.bfloat16)
    rest = value - high.astype(jnp.float32)
    middle = rest.astype(jnp.bfloat16)
    low = (rest - middle.astype(jnp.float32)).astype(jnp.bfloat16)
    return [part.astype(jnp.float32) for part in (high, middle, low)]


def columns(parts, rows):
    lane = lax.broadcasted_iota(jnp.int32, (rows, LANES), 1)
    out = jnp.zeros((rows, LANES), jnp.float32)
    for at, part in parts:
        out = jnp.where(lane == at, part, out)
    return out


def head_kernel(capacity, f_ids, b_ids, f_len, b_len, f_in, b_in, grad, gain, router, rows, f_pack, b_pack):
    tok_count = f_in.shape[0]

    def place(ids):
        chosen = jnp.where(ids[...] == 0, 1.0, 0.0)
        chosen = jnp.broadcast_to(chosen, (capacity, tok_count))
        before = lax.broadcasted_iota(jnp.int32, (tok_count, tok_count), 0)
        after = lax.broadcasted_iota(jnp.int32, (tok_count, tok_count), 1)
        upto = jnp.where(before <= after, 1.0, 0.0).astype(jnp.bfloat16)
        rank = jnp.dot(chosen.astype(jnp.bfloat16), upto, preferred_element_type=jnp.float32)
        slot = lax.broadcasted_iota(jnp.int32, (capacity, tok_count), 0).astype(jnp.float32)
        return jnp.where((rank - 1.0 == slot) & (chosen > 0.0), 1.0, 0.0)

    def side(ids, length, tokens):
        placing = place(ids)
        position = lax.broadcasted_iota(jnp.int32, (capacity, tok_count), 1)
        mask = jnp.sum(jnp.where(position < length[0, 0], placing, 0.0), axis=1, keepdims=True)
        values = jnp.dot(
            placing.astype(jnp.bfloat16), tokens[...], preferred_element_type=jnp.float32
        )
        inv = lax.rsqrt(jnp.mean(values * values, axis=1, keepdims=True) + EPS)
        normed = (values * inv * gain[...]).astype(jnp.bfloat16).astype(jnp.float32)
        logit = jnp.sum(normed * router[...].astype(jnp.float32), axis=1, keepdims=True)
        prob = 1.0 / (1.0 + jnp.exp(-logit))
        return placing, mask, values, inv, normed, prob

    def lanes_of(placing, scalars):
        parts = []
        for at, scalar in enumerate(scalars):
            parts += [(tok_count + 3 * at + i, part) for i, part in enumerate(split3(scalar))]
        wide = jnp.concatenate([placing, jnp.zeros((capacity, LANES - tok_count), jnp.float32)], axis=1)
        return wide + columns(parts, capacity)

    placing, mask, values, inv, normed, prob = side(b_ids, b_len, b_in)
    grads = jnp.dot(placing.astype(jnp.bfloat16), grad[...], preferred_element_type=jnp.float32)
    gain_parts = split3(gain[...])
    router32 = router[...].astype(jnp.float32)
    width = values.shape[1]
    meta = jnp.concatenate([values] + gain_parts + [router32, jnp.zeros((4, width), jnp.float32)], axis=0)
    b_lanes = lanes_of(placing, (prob, inv, mask * prob * (1.0 - prob)))
    b_pack[:tok_count, :width] = grad[...]
    b_pack[tok_count:, :width] = meta.astype(jnp.bfloat16)
    b_pack[:tok_count, width:] = jnp.zeros((tok_count, LANES), jnp.bfloat16)
    b_pack[tok_count:, width:] = jnp.concatenate([b_lanes, jnp.zeros_like(b_lanes)], axis=0).astype(jnp.bfloat16)
    f_placing, f_mask, f_values, f_inv, f_normed, f_prob = side(f_ids, f_len, f_in)
    rows[...] = jnp.concatenate([normed, grads * mask, f_normed], axis=0).astype(jnp.bfloat16)
    f_lanes = lanes_of(f_placing, (f_mask * f_prob,))
    f_pack[:, :width] = f_in[...]
    f_pack[:, width:] = jnp.concatenate(
        [f_lanes, jnp.zeros((tok_count - capacity, LANES), jnp.float32)], axis=0
    ).astype(jnp.bfloat16)


def fetched_head_kernel(capacity, f_len, b_len, *refs):
    count = 7
    sources, outs, held, arrived = refs[:count], refs[count : count + 3], refs[count + 3 : -1], refs[-1]
    copies = [
        pltpu.make_async_copy(source, target, arrived.at[at])
        for at, (source, target) in enumerate(zip(sources, held))
    ]
    for copy in copies:
        copy.start()
    for copy in copies:
        copy.wait()
    f_ids, b_ids, *tokens = held
    head_kernel(capacity, f_ids, b_ids, f_len, b_len, *tokens, *outs)


def head(capacity, f_ids, b_ids, f_len, b_len, f_in, b_in, grad, gain, router):
    tok_count, width = f_in.shape
    sources = (f_ids, b_ids, f_in, b_in, grad, gain, router)
    return pl.pallas_call(
        lambda *refs: fetched_head_kernel(capacity, *refs),
        out_shape=(
            jax.ShapeDtypeStruct((3 * capacity, width), jnp.bfloat16),
            jax.ShapeDtypeStruct((tok_count, width + LANES), jnp.bfloat16),
            jax.ShapeDtypeStruct((tok_count + 2 * capacity, width + LANES), jnp.bfloat16),
        ),
        in_specs=[SMEM, SMEM] + [pl.BlockSpec(memory_space=pl.ANY)] * len(sources),
        out_specs=(VMEM,) * 3,
        scratch_shapes=[pltpu.VMEM(source.shape, source.dtype) for source in sources]
        + [pltpu.SemaphoreType.DMA((len(sources),))],
        compiler_params=pltpu.CompilerParams(vmem_limit_bytes=56 * 1024 * 1024),
        name="head",
    )(f_len, b_len, *sources)


def sigmoid(value):
    return 1.0 / (1.0 + jnp.exp(-value))


def dot_t(left, right):
    return lax.dot_general(left, right, NT, preferred_element_type=jnp.float32)


def dot(left, right):
    return jnp.dot(left, right, preferred_element_type=jnp.float32)


def chunk_of(step, weights):
    part = weights[0].shape[0] // CHUNKS
    return [weight[step * part : (step + 1) * part] for weight in weights]


def forward_kernel(own, other, after, gate_w, up_w, down_w, mine, theirs, rows, total):
    half = own.shape[0]
    rows[:half] = own[...]
    rows[half:] = other[...]
    for step in range(CHUNKS):
        gate, up, down = chunk_of(step, (gate_w, up_w, down_w))
        gate_pre = dot_t(rows[...], gate)
        up_pre = dot_t(rows[...], up)
        hidden = (gate_pre * sigmoid(gate_pre) * up_pre).astype(jnp.bfloat16)
        if step == 0:
            total[...] = dot(hidden, down)
        elif step < CHUNKS - 1:
            total[...] += dot(hidden, down)
        else:
            part = total[...] + dot(hidden, down)
            mine[...] = part[:half]
            theirs[...] = part[half:].astype(jnp.bfloat16)


def backward_kernel(capacity, groups, after, gate_w, up_w, down_w, mine, theirs, rows, grads, total):
    half, width = mine.shape[0], rows.shape[1]
    pair = 2 * capacity
    blocks = [(ref, at) for ref in groups for at in range(0, ref.shape[0], pair)]
    for at in range(0, len(blocks), 2):
        low, high = [ref[start : start + pair].astype(jnp.float32) for ref, start in blocks[at : at + 2]]
        place = slice(at * capacity, at * capacity + pair)
        rows[place] = jnp.concatenate([low[:capacity], high[:capacity]], axis=0).astype(jnp.bfloat16)
        grads[place] = jnp.concatenate([low[capacity:], high[capacity:]], axis=0).astype(jnp.bfloat16)

    dots = jnp.zeros((2 * half, 1), jnp.float32)
    for step in range(CHUNKS):
        gate, up, down = chunk_of(step, (gate_w, up_w, down_w))
        gate_pre = dot_t(rows[...], gate)
        up_pre = dot_t(rows[...], up)
        d_hidden = dot_t(grads[...], down)
        gate_sig = sigmoid(gate_pre)
        silu = gate_pre * gate_sig
        hidden = (silu * up_pre).astype(jnp.bfloat16).astype(jnp.float32)
        dots += jnp.sum(hidden * d_hidden, axis=1, keepdims=True)
        d_gate = (d_hidden * up_pre * gate_sig * (1.0 + gate_pre * (1.0 - gate_sig))).astype(jnp.bfloat16)
        d_up = (d_hidden * silu).astype(jnp.bfloat16)
        part = dot(d_gate, gate) + dot(d_up, up)
        if step == 0:
            total[...] = part
        elif step < CHUNKS - 1:
            total[...] += part
        else:
            part += total[...]
            mine[:, :width] = part[:half]
            theirs[:, :width] = part[half:].astype(jnp.bfloat16)
    high = dots.astype(jnp.bfloat16).astype(jnp.float32)
    tail = columns([(0, high), (1, dots - high)], 2 * half)
    mine[:, width:] = tail[:half]
    theirs[:, width:] = tail[half:].astype(jnp.bfloat16)


def expert_call(kernel, name, operands, weights, extra, count, spaces, products, scratch):
    hidden, width = weights[0].shape
    half = count // 2
    return pl.pallas_call(
        kernel,
        out_shape=(
            jax.ShapeDtypeStruct((half, width + extra), jnp.float32),
            jax.ShapeDtypeStruct((half, width + extra), jnp.bfloat16),
        ),
        in_specs=spaces + [VMEM] * 3,
        out_specs=(VMEM, VMEM),
        scratch_shapes=[pltpu.VMEM((count, width), jnp.bfloat16)] * scratch
        + [pltpu.VMEM((count, width), jnp.float32)],
        compiler_params=pltpu.CompilerParams(vmem_limit_bytes=VMEM_LIMIT),
        cost_estimate=pl.CostEstimate(
            flops=products * 2 * count * hidden * width, bytes_accessed=6 * hidden * width, transcendentals=0
        ),
        name=name,
    )(*operands, *weights)


def hold(after, weights):
    def kernel(*refs):
        held = refs[-1]
        held[...] = jnp.zeros_like(held)

    return pl.pallas_call(
        kernel,
        out_shape=jax.ShapeDtypeStruct((8, LANES), jnp.float32),
        in_specs=[pl.BlockSpec(memory_space=pl.ANY)] * len(after) + [VMEM] * 3,
        out_specs=VMEM,
        compiler_params=pltpu.CompilerParams(vmem_limit_bytes=2 * 1024 * 1024),
        cost_estimate=pl.CostEstimate(
            flops=0, bytes_accessed=6 * weights[0].shape[0] * weights[0].shape[1], transcendentals=0
        ),
        name="hold",
    )(*after, *weights)


def forward_expert(own, other, after, weights):
    spaces = [VMEM, VMEM, pl.BlockSpec(memory_space=pl.ANY)]
    return expert_call(
        forward_kernel, "forward_expert", (own, other, after), weights, 0, 2 * own.shape[0], spaces, 3, 1
    )


def backward_expert(capacity, groups, after, weights):
    count = sum(group.shape[0] for group in groups) // 2

    def kernel(*refs):
        backward_kernel(capacity, refs[: len(groups)], *refs[len(groups) :])

    return expert_call(
        kernel,
        "backward_expert",
        groups + [after],
        weights,
        LANES,
        count,
        [VMEM] * len(groups) + [pl.BlockSpec(memory_space=pl.ANY)],
        5,
        2,
    )


def scalar_of(lanes, tok_count, at):
    first = tok_count + 3 * at
    return lanes[:, first : first + 1] + lanes[:, first + 1 : first + 2] + lanes[:, first + 2 : first + 3]


def overlay(placing, rows, tokens, out):
    place16 = placing.astype(jnp.bfloat16)
    placed = lax.dot_general(place16, rows.astype(jnp.bfloat16), TN, preferred_element_type=jnp.float32)
    ones = jnp.ones((placing.shape[0], LANES), jnp.bfloat16)
    chosen = lax.dot_general(place16, ones, TN, preferred_element_type=jnp.float32)
    out[...] = jnp.where(chosen[:, :1] > 0.0, placed, tokens[...].astype(jnp.float32)).astype(jnp.bfloat16)


def forward_finish_kernel(capacity, sums, pack, out):
    tok_count, width = out.shape
    lanes = pack[:, width:].astype(jnp.float32)[:capacity]
    placing = lanes[:, :tok_count]
    tokens = pack[:, :width]
    values = dot(placing.astype(jnp.bfloat16), tokens)
    result = sums[...].astype(jnp.bfloat16).astype(jnp.float32)
    overlay(placing, values + scalar_of(lanes, tok_count, 0) * result, tokens, out)


def backward_finish_kernel(capacity, sums, pack, out):
    tok_count, width = out.shape
    lanes = pack[tok_count:, width:].astype(jnp.float32)[:capacity]
    wide = pack[tok_count:, :width].astype(jnp.float32)
    tokens = pack[:tok_count, :width]
    values = wide[:capacity]
    gain = wide[capacity : capacity + 1] + wide[capacity + 1 : capacity + 2] + wide[capacity + 2 : capacity + 3]
    router = wide[capacity + 3 : capacity + 4]
    placing = lanes[:, :tok_count]
    prob, inv, slope = [scalar_of(lanes, tok_count, at) for at in range(3)]
    grads = dot(placing.astype(jnp.bfloat16), tokens)
    d_rows = sums[:, :width].astype(jnp.bfloat16).astype(jnp.float32)
    row_dot = sums[:, width : width + 1] + sums[:, width + 1 : width + 2]
    weighted = gain * (prob * d_rows + (slope * row_dot) * router)
    inner = jnp.mean(weighted * values, axis=1, keepdims=True)
    overlay(placing, grads + inv * weighted - values * inv * inv * inv * inner, tokens, out)


def finish(kernel, name, capacity, sums, pack, tok_count):
    return pl.pallas_call(
        lambda *refs: kernel(capacity, *refs),
        out_shape=jax.ShapeDtypeStruct((tok_count, pack.shape[1] - LANES), pack.dtype),
        in_specs=[VMEM, VMEM],
        out_specs=VMEM,
        compiler_params=pltpu.CompilerParams(vmem_limit_bytes=8 * 1024 * 1024),
        name=name,
    )(sums, pack)


def gather_column(own):
    half = own.shape[1] // (2 * LANES) * LANES
    below2 = along_z(own, 2)
    above2 = along_z(own, -2)
    below1 = along_z(own, 1)
    above1 = along_z(own, -1)
    below3 = along_z(below2, 1)
    above3 = along_z(above2, -1)
    far_low = along_z(below2[:, :half], 2)
    far_high = along_z(above2[:, half:], -2)
    far = jnp.concatenate([far_low, far_high], axis=1)
    return [own], [below1, above1], [below2, above2], [below3, above3, far]


def sum_columns(b_total, f_total, capacity, packs):
    width = b_total.shape[1]
    low, full = jnp.bfloat16, jnp.float32
    total = jnp.concatenate([b_total, f_total], axis=1)
    own, below1, above1, below2, above2, below3, above3, far = [
        total[at * capacity : (at + 1) * capacity] for at in range(total.shape[0] // capacity)
    ]
    both = total.shape[1]
    up = along_z(jnp.concatenate([above1, below2, far[:, :width]], axis=1).astype(low), 1)
    down = along_z(jnp.concatenate([below1, above2, far[:, width:]], axis=1).astype(low), -1)
    up, down, *packs = lax.optimization_barrier((up, down, *packs))
    up, down = up.astype(full), down.astype(full)
    near = own + up[:, :both] + down[:, :both]
    above3 = above3 + down[:, both : 2 * both]
    below3 = below3 + up[:, both : 2 * both]
    b_up = across((above3[:, :width] + up[:, 2 * both :]).astype(low), -1, 3)
    b_down = across(below3[:, :width].astype(low), -1, -3)
    f_up = across(above3[:, width:].astype(low), 1, 3)
    f_down = across((below3[:, width:] + down[:, 2 * both :]).astype(low), 1, -3)
    b_near = across(near[:, :width].astype(low), -1, 0)
    f_near = across(near[:, width:].astype(low), 1, 0)

    def add(parts):
        return sum(part.astype(full) for part in parts)

    return add((b_near, b_up, b_down)), add((f_near, f_up, f_down)), *packs


def body(
    fwd_in,
    fwd_ids,
    fwd_lengths,
    bwd_in,
    bwd_grad,
    bwd_ids,
    bwd_lengths,
    norm_gain,
    router,
    w_gate,
    w_up,
    w_down,
):
    tok_count = fwd_in.shape[1]
    capacity = max(2, 2 * tok_count // EXPERTS)
    weights = (w_gate[0].T, w_up[0].T, w_down[0])

    rows, f_pack, b_pack = head(
        capacity, fwd_ids, bwd_ids, fwd_lengths, bwd_lengths, fwd_in[0], bwd_in[0], bwd_grad[0], norm_gain, router
    )
    column = gather_column(rows)
    other = swap_x(rows)
    other_near = [along_z(other, 1), along_z(other, -1)]
    pair = 2 * capacity

    def of_backward(blocks):
        return jnp.concatenate([block[:pair] for block in blocks], axis=0)

    def of_forward(blocks):
        return jnp.concatenate([block[pair:] for block in blocks], axis=0)

    own, near, two, far = column
    groups = [of_backward(blocks) for blocks in column]
    other_two = swap_x(jnp.concatenate(two, axis=0))
    other_two = [other_two[: 3 * capacity], other_two[3 * capacity :]]
    others = [of_backward([other]), of_backward(other_near), of_backward(other_two), swap_x(groups[3])]
    f_own = of_forward(own + near + two + far)
    loaded = hold((groups[3],), weights)
    f_far, others[3], loaded = lax.optimization_barrier((of_forward(far), others[3], loaded))
    f_other = jnp.concatenate([of_forward([other] + other_near + other_two), swap_x(f_far)], axis=0)

    b_mine, b_theirs = backward_expert(capacity, groups + others, loaded, weights)
    f_mine, f_theirs = forward_expert(f_own, f_other, b_theirs, weights)
    b_got, f_pack, b_pack = lax.optimization_barrier((swap_x(b_theirs), f_pack, b_pack))
    packs = (across(f_pack, 1, 0), across(b_pack, -1, 0))
    b_total = b_mine + b_got.astype(jnp.float32)
    f_total = f_mine + swap_x(f_theirs).astype(jnp.float32)
    b_sums, f_sums, f_pack, b_pack = sum_columns(b_total, f_total, capacity, packs)
    bwd_out = finish(backward_finish_kernel, "backward_finish", capacity, b_sums, b_pack, tok_count)
    fwd_out = finish(forward_finish_kernel, "forward_finish", capacity, f_sums, f_pack, tok_count)
    return (fwd_out[None], bwd_out[None])


def solution(mesh):
    in_specs = (
        P("pipe", "dp", None),
        P("pipe", "dp"),
        P("pipe", "dp"),
        P("pipe", "dp", None),
        P("pipe", "dp", None),
        P("pipe", "dp"),
        P("pipe", "dp"),
        P("pipe", None),
        P("pipe", None),
        P("pipe", None, "dp"),
        P("pipe", None, "dp"),
        P("pipe", "dp", None),
    )
    out_specs = (P("pipe", "dp", None), P("pipe", "dp", None))
    return jax.shard_map(body, mesh=mesh, in_specs=in_specs, out_specs=out_specs, check_vma=False)
```

```python
import jax
import jax.numpy as jnp
from jax import lax
from jax.experimental import pallas as pl
from jax.experimental.pallas import tpu as pltpu
from jax.sharding import PartitionSpec as P

EXPERTS = 16
EPS = 1e-05
LANES = 128
CHUNKS = 1
VMEM_LIMIT = 20 * 1024 * 1024
VMEM = pl.BlockSpec(memory_space=pltpu.VMEM)
SMEM = pl.BlockSpec(memory_space=pltpu.SMEM)
NT = (((1,), (1,)), ((), ()))
TN = (((0,), (0,)), ((), ()))


def along_z(value, steps):
    count = lax.axis_size("dp")
    pairs = [(source, (source + 2 * steps) % count) for source in range(count)]
    return lax.ppermute(value, "dp", pairs)


def swap_x(value):
    count = lax.axis_size("dp")
    return lax.ppermute(value, "dp", [(source, source ^ 1) for source in range(count)])


def across(value, stages, steps):
    n_pipe, n_dp = lax.axis_size("pipe"), lax.axis_size("dp")
    pairs = [
        (p * n_dp + d, (p + stages) % n_pipe * n_dp + (d + 2 * steps) % n_dp)
        for p in range(n_pipe)
        for d in range(n_dp)
    ]
    return lax.ppermute(value, ("pipe", "dp"), pairs)


def columns(parts, rows):
    lane = lax.broadcasted_iota(jnp.int32, (rows, LANES), 1)
    out = jnp.zeros((rows, LANES), jnp.float32)
    for at, part in parts:
        out = jnp.where(lane == at, part, out)
    return out


def place(ids, capacity):
    tok_count = ids.shape[1]
    chosen = jnp.broadcast_to(jnp.where(ids == 0, 1.0, 0.0), (capacity, tok_count))
    before = lax.broadcasted_iota(jnp.int32, (tok_count, tok_count), 0)
    after = lax.broadcasted_iota(jnp.int32, (tok_count, tok_count), 1)
    upto = jnp.where(before <= after, 1.0, 0.0).astype(jnp.bfloat16)
    rank = dot(chosen.astype(jnp.bfloat16), upto)
    slot = lax.broadcasted_iota(jnp.int32, (capacity, tok_count), 0).astype(jnp.float32)
    return jnp.where((rank - 1.0 == slot) & (chosen > 0.0), 1.0, 0.0)


def slot_mask(placing, length):
    position = lax.broadcasted_iota(jnp.int32, placing.shape, 1)
    return jnp.sum(jnp.where(position < length, placing, 0.0), axis=1, keepdims=True)


def normalize(placing, tokens, gain):
    values = dot(placing.astype(jnp.bfloat16), tokens)
    inv = lax.rsqrt(jnp.mean(values * values, axis=1, keepdims=True) + EPS)
    return values, inv, (values * inv * gain).astype(jnp.bfloat16).astype(jnp.float32)


def head_kernel(capacity, f_len, b_len, *refs):
    sources, (rows, f_side, b_side), held, arrived = refs[:7], refs[7:10], refs[10:17], refs[17]
    copies = [
        pltpu.make_async_copy(source, target, arrived.at[at])
        for at, (source, target) in enumerate(zip(sources, held))
    ]
    for copy in copies:
        copy.start()
    for copy in copies:
        copy.wait()
    f_ids, b_ids, gain, router, f_in, b_in, grad = [ref[...] for ref in held]
    router = router.astype(jnp.float32)
    tok_count, width = f_in.shape

    def side(ids, length, tokens):
        placing = place(ids, capacity)
        values, inv, normed = normalize(placing, tokens, gain)
        prob = sigmoid(jnp.sum(normed * router, axis=1, keepdims=True))
        return placing, slot_mask(placing, length[0, 0]), values, inv, normed, prob

    def lanes_of(placing, scalars):
        wide = jnp.concatenate([placing, jnp.zeros((capacity, LANES - tok_count), jnp.float32)], axis=1)
        return wide + columns([(tok_count + at, scalar) for at, scalar in enumerate(scalars)], capacity)

    placing, mask, values, inv, normed, prob = side(b_ids, b_len, b_in)
    grads = dot(placing.astype(jnp.bfloat16), grad)
    b_rows = [normed, grads * mask]
    b_side[:capacity, :width] = values
    b_side[capacity : 2 * capacity, :width] = grads
    b_side[2 * capacity :, :width] = jnp.concatenate(
        [gain, router, jnp.zeros((capacity - 2, width), jnp.float32)], axis=0
    )
    b_side[:capacity, width:] = lanes_of(placing, (prob, inv, mask * prob * (1.0 - prob)))
    b_side[capacity:, width:] = jnp.zeros((2 * capacity, LANES), jnp.float32)
    placing, mask, values, inv, normed, prob = side(f_ids, f_len, f_in)
    rows[...] = jnp.concatenate(b_rows + [normed], axis=0).astype(jnp.bfloat16)
    f_side[:, :width] = values
    f_side[:, width:] = lanes_of(placing, (mask * prob,))


def head(capacity, f_len, b_len, *sources):
    width = sources[-1].shape[1]
    return pl.pallas_call(
        lambda *refs: head_kernel(capacity, *refs),
        out_shape=(
            jax.ShapeDtypeStruct((3 * capacity, width), jnp.bfloat16),
            jax.ShapeDtypeStruct((capacity, width + LANES), jnp.float32),
            jax.ShapeDtypeStruct((3 * capacity, width + LANES), jnp.float32),
        ),
        in_specs=[SMEM, SMEM] + [pl.BlockSpec(memory_space=pl.ANY)] * len(sources),
        out_specs=(VMEM,) * 3,
        scratch_shapes=[pltpu.VMEM(source.shape, source.dtype) for source in sources]
        + [pltpu.SemaphoreType.DMA((len(sources),))],
        compiler_params=pltpu.CompilerParams(vmem_limit_bytes=56 * 1024 * 1024),
        name="head",
    )(f_len, b_len, *sources)


def sigmoid(value):
    return 1.0 / (1.0 + jnp.exp(-value))


def dot_t(left, right):
    return lax.dot_general(left, right, NT, preferred_element_type=jnp.float32)


def dot(left, right):
    return jnp.dot(left, right, preferred_element_type=jnp.float32)


def chunk_of(step, weights):
    part = weights[0].shape[0] // CHUNKS
    return [weight[step * part : (step + 1) * part] for weight in weights]


def forward_kernel(own, other, after, gate_w, up_w, down_w, mine, theirs, rows, total):
    half = own.shape[0]
    rows[:half] = own[...]
    rows[half:] = other[...]
    for step in range(CHUNKS):
        gate, up, down = chunk_of(step, (gate_w, up_w, down_w))
        gate_pre = dot_t(rows[...], gate)
        up_pre = dot_t(rows[...], up)
        hidden = (gate_pre * sigmoid(gate_pre) * up_pre).astype(jnp.bfloat16)
        if step == 0 and CHUNKS > 1:
            total[...] = dot(hidden, down)
        elif step < CHUNKS - 1:
            total[...] += dot(hidden, down)
        else:
            part = (total[...] if step else 0.0) + dot(hidden, down)
            mine[...] = part[:half]
            theirs[...] = part[half:].astype(jnp.bfloat16)


def backward_kernel(capacity, groups, after, gate_w, up_w, down_w, mine, theirs, rows, grads, total):
    half, width = mine.shape[0], rows.shape[1]
    pair = 2 * capacity
    blocks = [(ref, at) for ref in groups for at in range(0, ref.shape[0], pair)]
    for at in range(0, len(blocks), 2):
        low, high = [ref[start : start + pair].astype(jnp.float32) for ref, start in blocks[at : at + 2]]
        place = slice(at * capacity, at * capacity + pair)
        rows[place] = jnp.concatenate([low[:capacity], high[:capacity]], axis=0).astype(jnp.bfloat16)
        grads[place] = jnp.concatenate([low[capacity:], high[capacity:]], axis=0).astype(jnp.bfloat16)

    dots = jnp.zeros((2 * half, 1), jnp.float32)
    for step in range(CHUNKS):
        gate, up, down = chunk_of(step, (gate_w, up_w, down_w))
        gate_pre = dot_t(rows[...], gate)
        up_pre = dot_t(rows[...], up)
        d_hidden = dot_t(grads[...], down)
        gate_sig = sigmoid(gate_pre)
        silu = gate_pre * gate_sig
        hidden = (silu * up_pre).astype(jnp.bfloat16).astype(jnp.float32)
        dots += jnp.sum(hidden * d_hidden, axis=1, keepdims=True)
        d_gate = (d_hidden * up_pre * gate_sig * (1.0 + gate_pre * (1.0 - gate_sig))).astype(jnp.bfloat16)
        d_up = (d_hidden * silu).astype(jnp.bfloat16)
        part = dot(d_gate, gate) + dot(d_up, up)
        if step == 0 and CHUNKS > 1:
            total[...] = part
        elif step < CHUNKS - 1:
            total[...] += part
        else:
            part += total[...] if step else 0.0
            mine[:, :width] = part[:half]
            theirs[:, :width] = part[half:].astype(jnp.bfloat16)
    high = dots.astype(jnp.bfloat16).astype(jnp.float32)
    tail = columns([(0, high), (1, dots - high)], 2 * half)
    mine[:, width:] = tail[:half]
    theirs[:, width:] = tail[half:].astype(jnp.bfloat16)


def expert_call(kernel, name, operands, weights, extra, count, spaces, products, scratch):
    hidden, width = weights[0].shape
    half = count // 2
    return pl.pallas_call(
        kernel,
        out_shape=(
            jax.ShapeDtypeStruct((half, width + extra), jnp.float32),
            jax.ShapeDtypeStruct((half, width + extra), jnp.bfloat16),
        ),
        in_specs=spaces + [VMEM] * 3,
        out_specs=(VMEM, VMEM),
        scratch_shapes=[pltpu.VMEM((count, width), jnp.bfloat16)] * scratch
        + [pltpu.VMEM((count, width), jnp.float32)],
        compiler_params=pltpu.CompilerParams(vmem_limit_bytes=VMEM_LIMIT),
        cost_estimate=pl.CostEstimate(
            flops=products * 2 * count * hidden * width, bytes_accessed=6 * hidden * width, transcendentals=0
        ),
        name=name,
    )(*operands, *weights)


def hold(after, weights):
    def kernel(*refs):
        held = refs[-1]
        held[...] = jnp.zeros_like(held)

    return pl.pallas_call(
        kernel,
        out_shape=jax.ShapeDtypeStruct((8, LANES), jnp.float32),
        in_specs=[pl.BlockSpec(memory_space=pl.ANY)] * len(after) + [VMEM] * 3,
        out_specs=VMEM,
        compiler_params=pltpu.CompilerParams(vmem_limit_bytes=2 * 1024 * 1024),
        cost_estimate=pl.CostEstimate(
            flops=0, bytes_accessed=6 * weights[0].shape[0] * weights[0].shape[1], transcendentals=0
        ),
        name="hold",
    )(*after, *weights)


def forward_expert(own, other, after, weights):
    spaces = [VMEM, VMEM, pl.BlockSpec(memory_space=pl.ANY)]
    return expert_call(
        forward_kernel, "forward_expert", (own, other, after), weights, 0, 2 * own.shape[0], spaces, 3, 1
    )


def backward_expert(capacity, groups, after, weights):
    count = sum(group.shape[0] for group in groups) // 2

    def kernel(*refs):
        backward_kernel(capacity, refs[: len(groups)], *refs[len(groups) :])

    return expert_call(
        kernel,
        "backward_expert",
        groups + [after],
        weights,
        LANES,
        count,
        [VMEM] * len(groups) + [pl.BlockSpec(memory_space=pl.ANY)],
        5,
        2,
    )


def overlay(placing, rows, tokens, out):
    place16 = placing.astype(jnp.bfloat16)
    placed = lax.dot_general(place16, rows.astype(jnp.bfloat16), TN, preferred_element_type=jnp.float32)
    ones = jnp.ones((placing.shape[0], LANES), jnp.bfloat16)
    chosen = lax.dot_general(place16, ones, TN, preferred_element_type=jnp.float32)
    out[...] = jnp.where(chosen[:, :1] > 0.0, placed, tokens[...].astype(jnp.float32)).astype(jnp.bfloat16)


def rows_kernel(tok_count, near, up, down, f_side, b_side, f_out, b_out):
    capacity, width = near.shape[0], f_side.shape[1] - LANES
    total = near[...] + up[...].astype(jnp.float32) + down[...].astype(jnp.float32)
    d_rows = total[:, :width].astype(jnp.bfloat16).astype(jnp.float32)
    row_dot = total[:, width : width + 1] + total[:, width + 1 : width + 2]
    result = total[:, width + LANES :].astype(jnp.bfloat16).astype(jnp.float32)
    values, grads = b_side[:capacity, :width], b_side[capacity : 2 * capacity, :width]
    gain = b_side[2 * capacity : 2 * capacity + 1, :width]
    router = b_side[2 * capacity + 1 : 2 * capacity + 2, :width]
    lanes = b_side[:capacity, width:]
    prob, inv, slope = [lanes[:, tok_count + at : tok_count + at + 1] for at in range(3)]
    weighted = gain * (prob * d_rows + (slope * row_dot) * router)
    inner = jnp.mean(weighted * values, axis=1, keepdims=True)
    b_out[:, :width] = (grads + inv * weighted - values * inv * inv * inv * inner).astype(jnp.bfloat16)
    b_out[:, width:] = lanes.astype(jnp.bfloat16)
    scale = f_side[:, width + tok_count : width + tok_count + 1]
    f_out[:, :width] = (f_side[:, :width] + scale * result).astype(jnp.bfloat16)
    f_out[:, width:] = f_side[:, width:].astype(jnp.bfloat16)


def finished_rows(tok_count, near, up, down, f_side, b_side):
    return pl.pallas_call(
        lambda *refs: rows_kernel(tok_count, *refs),
        out_shape=(jax.ShapeDtypeStruct(f_side.shape, jnp.bfloat16),) * 2,
        in_specs=[VMEM] * 5,
        out_specs=(VMEM, VMEM),
        compiler_params=pltpu.CompilerParams(vmem_limit_bytes=8 * 1024 * 1024),
        name="rows",
    )(near, up, down, f_side, b_side)


def finish_kernel(moved, tokens, out):
    tok_count, width = tokens.shape
    overlay(moved[:, width : width + tok_count].astype(jnp.float32), moved[:, :width], tokens[...], out)


def finish(moved, tokens):
    return pl.pallas_call(
        finish_kernel,
        out_shape=jax.ShapeDtypeStruct(tokens.shape, tokens.dtype),
        in_specs=[VMEM, VMEM],
        out_specs=VMEM,
        compiler_params=pltpu.CompilerParams(vmem_limit_bytes=8 * 1024 * 1024),
        name="finish",
    )(moved, tokens)


def gather_column(own):
    half = own.shape[1] // (2 * LANES) * LANES
    below2 = along_z(own, 2)
    above2 = along_z(own, -2)
    below1 = along_z(own, 1)
    above1 = along_z(own, -1)
    below3 = along_z(below2, 1)
    above3 = along_z(above2, -1)
    far_low = along_z(below2[:, :half], 2)
    far_high = along_z(above2[:, half:], -2)
    far = jnp.concatenate([far_low, far_high], axis=1)
    return [own], [below1, above1], [below2, above2], [below3, above3, far]


def sum_columns(b_total, f_total, capacity, tokens):
    width = b_total.shape[1]
    low, full = jnp.bfloat16, jnp.float32
    total = jnp.concatenate([b_total, f_total], axis=1)
    own, below1, above1, below2, above2, below3, above3, far = [
        total[at * capacity : (at + 1) * capacity] for at in range(total.shape[0] // capacity)
    ]
    both = total.shape[1]
    up = along_z(jnp.concatenate([above1, below2, far[:, :width]], axis=1).astype(low), 1)
    down = along_z(jnp.concatenate([below1, above2, far[:, width:]], axis=1).astype(low), -1)
    up, down = up.astype(full), down.astype(full)
    near = own + up[:, :both] + down[:, :both]
    above3 = above3 + down[:, both : 2 * both]
    below3 = below3 + up[:, both : 2 * both]
    above3 = jnp.concatenate([above3[:, :width] + up[:, 2 * both :], above3[:, width:]], axis=1)
    below3 = jnp.concatenate([below3[:, :width], below3[:, width:] + down[:, 2 * both :]], axis=1)
    return (near, along_z(above3.astype(low), 3), along_z(below3.astype(low), -3)), tokens


def body(
    fwd_in,
    fwd_ids,
    fwd_lengths,
    bwd_in,
    bwd_grad,
    bwd_ids,
    bwd_lengths,
    norm_gain,
    router,
    w_gate,
    w_up,
    w_down,
):
    tok_count = fwd_in.shape[1]
    capacity = max(2, 2 * tok_count // EXPERTS)
    weights = (w_gate[0].T, w_up[0].T, w_down[0])

    rows, f_side, b_side = head(
        capacity, fwd_lengths, bwd_lengths, fwd_ids, bwd_ids, norm_gain, router, fwd_in[0], bwd_in[0], bwd_grad[0]
    )
    column = gather_column(rows)
    other = swap_x(rows)
    other_near = [along_z(other, 1), along_z(other, -1)]
    pair = 2 * capacity

    def of_backward(blocks):
        return jnp.concatenate([block[:pair] for block in blocks], axis=0)

    def of_forward(blocks):
        return jnp.concatenate([block[pair:] for block in blocks], axis=0)

    own, near, two, far = column
    groups = [of_backward(blocks) for blocks in column]
    other_two = swap_x(jnp.concatenate(two, axis=0))
    other_two = [other_two[: 3 * capacity], other_two[3 * capacity :]]
    others = [of_backward([other]), of_backward(other_near), of_backward(other_two), swap_x(groups[3])]
    f_own = of_forward(own + near + two + far)
    loaded = hold((groups[3],), weights)
    f_far, others[3], loaded = lax.optimization_barrier((of_forward(far), others[3], loaded))
    f_other = jnp.concatenate([of_forward([other] + other_near + other_two), swap_x(f_far)], axis=0)

    b_mine, b_theirs = backward_expert(capacity, groups + others, loaded, weights)
    f_mine, f_theirs = forward_expert(f_own, f_other, b_theirs, weights)
    b_got = swap_x(b_theirs)
    b_total = b_mine + b_got.astype(jnp.float32)
    f_got, f_tokens, b_tokens = lax.optimization_barrier((swap_x(f_theirs), fwd_in[0], bwd_grad[0]))
    tokens = (across(f_tokens, 1, 0), across(b_tokens, -1, 0))
    f_total = f_mine + f_got.astype(jnp.float32)
    parts, (f_tokens, b_tokens) = sum_columns(b_total, f_total, capacity, tokens)
    f_done, b_done = finished_rows(tok_count, *parts, f_side, b_side)
    bwd_out = finish(across(b_done, -1, 0), b_tokens)
    fwd_out = finish(across(f_done, 1, 0), f_tokens)
    return (fwd_out[None], bwd_out[None])


def solution(mesh):
    in_specs = (
        P("pipe", "dp", None),
        P("pipe", "dp"),
        P("pipe", "dp"),
        P("pipe", "dp", None),
        P("pipe", "dp", None),
        P("pipe", "dp"),
        P("pipe", "dp"),
        P("pipe", None),
        P("pipe", None),
        P("pipe", None, "dp"),
        P("pipe", None, "dp"),
        P("pipe", "dp", None),
    )
    out_specs = (P("pipe", "dp", None), P("pipe", "dp", None))
    return jax.shard_map(body, mesh=mesh, in_specs=in_specs, out_specs=out_specs, check_vma=False)
```
